128 devices in a mesh: aux: 16 (over z, y), bas: 8 (over x, core).
Axes of the slice: x: 4, y: 4, z: 4, core: 2. Of those that a mesh axis runs over, the one named last changes fastest.
Arguments:
- tiles: bfloat16 [16384, 4, 32, 128], P(('aux', 'bas')), may hold values from -6 to 6
- tile_owner: int32 [16384, 1], replicated, may hold values from 0 to 127; in each aligned block of 128 rows (0 to 127, 128 to 255, ...) at most 2 rows name the same one
- pair_rows: int32 [16384], replicated, may hold values from 0 to 639
- pair_cols: int32 [16384], replicated, may hold values from 0 to 159
- orbitals: bfloat16 [32, 20480], replicated, may hold values from -0.5 to 0.5
- support: int32 [32, 160], replicated, may hold values 0 or 1
Outputs:
- exchange: float32 [20480, 20480], P('aux', 'bas')
The draws below stay inside these ranges and needn't reach their ends.
Inputs may be any that keep to these rules, and one draw needn't show every extreme that they name: tile_owner[t, 0] is the device that half-transforms tile t, numbered aux index times 8 plus bas index; the integrals of tile t belong to auxiliary block tile_owner[t, 0] // 8. Among the 128 rows of one device no value appears more than 2 times, and some value appears exactly 2 times.
All inputs are finite; a program needn't handle non-finite values.
Results may differ from the reference program's by a relative error of at most 0.0075.
Values may be sent and summed in bfloat16 or wider, within the bound.
No kernel may reach another device: no remote copies, remote signals or barrier semaphores. Data moves between devices by JAX's collectives and lax.ppermute only.
A program may use at most 128 MiB of HBM per device.

```python
import math
import jax
import jax.numpy as jnp
import numpy as np
from jax import lax

NBAS = 20480
OCC = 32
AUX_DEV = 4
TMU = 32
TNU = 128
TILE_DEV = 128
TILES = 16384
CAP = 2
N_AUX = 16
N_BAS = 8


def touch_ends(values, rng, low, top_value):
    dims = values.shape
    place = [jax.random.randint(jax.random.fold_in(rng, axis), (), 0, dims[axis]) for axis in range(len(dims))]
    values = values.at[tuple(place)].set(low)
    longest = dims.index(max(dims))
    place[longest] = (place[longest] + 1) % dims[longest]
    return values.at[tuple(place)].set(top_value)


def block_levels(rng, dims, pieces, low, high):
    factor_of, own = 1.0, jax.random.fold_in(rng, 6)
    for axis_at, blocks in pieces:
        heights = jnp.exp(jax.random.uniform(jax.random.fold_in(own, axis_at), (blocks,), jnp.float32, low / len(pieces), high / len(pieces)))
        factor_of = factor_of * jnp.repeat(heights, dims[axis_at] // blocks).reshape([-1 if axis == axis_at else 1 for axis in range(len(dims))])
    return factor_of


def routed_block(rng, own, number, rows, count, top, most, lean):
    ranking = jax.random.permutation(rng, count)
    heavy_load, common = shares(count, rows * top, most, lean, True), shares(count, rows * top, most, lean, False)
    places = jnp.arange(count)

    def named(lengths, offset_by):
        used = int((lengths > 0).sum())
        fixed = max(1, used // 4)
        moved = fixed + (places - fixed + offset_by * (used - fixed)) % max(1, count - fixed)
        return jnp.zeros((count,), jnp.int32).at[ranking[jnp.where(places < fixed, places, moved)]].set(jnp.asarray(lengths, jnp.int32))

    lengths = jnp.where(number % 4 == 0, named(heavy_load, number // 4), named(common, number - number // 4 - 1))
    mixed = jax.random.permutation(jax.random.fold_in(own, 3), count)
    donor, receiver = mixed[0:count // 2 * 2:2], mixed[1:count // 2 * 2:2]
    room = jnp.minimum(lengths[donor] - 1, most - lengths[receiver]) // 2
    room = jnp.where((donor == ranking[0]) | (receiver == ranking[0]) | (lengths[receiver] == 0), 0, jnp.maximum(room, 0))
    moved = jax.random.randint(jax.random.fold_in(own, 4), (count // 2,), 0, 1 << 20) % (room + 1)
    lengths = lengths.at[donor].add(-moved).at[receiver].add(moved)
    labels = jnp.searchsorted(jnp.cumsum(lengths), jnp.arange(rows * top), side="right").astype(jnp.int32)
    grid = labels.reshape(top, rows).T
    grid = grid[jax.random.permutation(jax.random.fold_in(own, 1), rows)]
    offset_by = jax.random.randint(jax.random.fold_in(own, 2), (rows, 1), 0, top)
    return jnp.take_along_axis(grid, (jnp.arange(top)[None, :] + offset_by) % top, axis=1)


def shares(number_of, total, reach, lean, full):
    weights = [(1 << 20) // math.isqrt(grade ** lean) + 1 for grade in range(1, number_of + 1)]
    largest = reach if full else min(reach, max(-(-total // number_of), total * weights[0] // sum(weights)))
    least = 1 if total - largest >= number_of - 1 else 0
    given, spare = [largest] + [least] * (number_of - 1), total - largest - least * (number_of - 1)
    while spare > 0:
        candidates = [i for i in range(1, number_of) if given[i] < largest] or [i for i in range(1, number_of) if given[i] < reach]
        pool, budget = sum([weights[i] for i in candidates]), spare
        for i in candidates:
            extra = min(reach - given[i], max(1, budget * weights[i] // pool), spare)
            given[i] = given[i] + extra
            spare = spare - extra
    return np.array(given)


def scatter_about(own_key, dims, deviation, most, shards=(), kind=jnp.bfloat16):
    drawn = deviation * jax.random.normal(own_key, dims, jnp.float32)
    if shards:
        drawn = drawn * block_levels(own_key, dims, shards, -0.22, 0.18)
    return jnp.clip(drawn, -most, most).astype(kind)


def setup_inputs(seed: int = 0) -> dict:
    arg_keys = jax.random.split(jax.random.key(seed), 7)
    tiles = scatter_about(arg_keys[0], (TILES, AUX_DEV, TMU, TNU), 1.0, 6.0, ((0, 128),))
    tile_owner_keys = jax.random.split(jax.random.fold_in(arg_keys[1], 1), TILES // TILE_DEV)
    tile_owner_turns = jax.random.permutation(jax.random.fold_in(arg_keys[1], 3), TILES // TILE_DEV)
    tile_owner = jax.vmap(lambda own, number: routed_block(jax.random.fold_in(arg_keys[1], 2), own, number, TILE_DEV, N_AUX * N_BAS, 1, CAP, 2))(tile_owner_keys, tile_owner_turns).reshape((TILES, 1))
    pair_rows = touch_ends(jax.random.randint(arg_keys[2], (TILES,), 0, NBAS // TMU), jax.random.fold_in(arg_keys[2], 1), 0, (NBAS // TMU) - 1).astype(jnp.int32)
    pair_cols = touch_ends(jax.random.randint(arg_keys[3], (TILES,), 0, NBAS // TNU), jax.random.fold_in(arg_keys[3], 1), 0, (NBAS // TNU) - 1).astype(jnp.int32)
    orbitals = scatter_about(arg_keys[4], (OCC, NBAS), TNU ** -0.5, 0.5)
    support = touch_ends((jax.random.randint(arg_keys[5], (OCC, NBAS // TNU), 0, 2) < 1).astype(jnp.int32), jax.random.fold_in(arg_keys[5], 1), 0, 1)
    return {"tiles": tiles, "tile_owner": tile_owner, "pair_rows": pair_rows, "pair_cols": pair_cols, "orbitals": orbitals, "support": support}


def masked_blocks(orbitals, support):
    block_count = support.shape[1]
    kept = jnp.repeat(support, TNU, axis=1) == 1
    coefficient = jnp.where(kept, orbitals, jnp.zeros_like(orbitals))
    return coefficient.reshape(OCC, block_count, TNU).transpose(1, 0, 2)


def reference(tiles, tile_owner, pair_rows, pair_cols, orbitals, support):
    devices = N_AUX * N_BAS
    width = AUX_DEV * OCC
    row_blocks = NBAS // TMU
    coefficient = masked_blocks(orbitals, support)

    def half_group(group):
        tile_group, col_group = group
        chosen = coefficient[col_group].astype(jnp.float32)
        product = jnp.einsum("kpmn,kin->kmpi", tile_group.astype(jnp.float32), chosen)
        return product.reshape(TILE_DEV, TMU, width).astype(jnp.bfloat16)

    halves = lax.map(half_group, (tiles.reshape(devices, TILE_DEV, AUX_DEV, TMU, TNU), pair_cols.reshape(devices, TILE_DEV)))
    halves = halves.reshape(devices * TILE_DEV, TMU, width).astype(jnp.float32)
    owner = tile_owner[:, 0]

    def aux_block(group_index):
        inside = owner // N_BAS == group_index
        segment = jnp.where(inside, (owner % N_BAS) * row_blocks + pair_rows, N_BAS * row_blocks)
        partial_value = jax.ops.segment_sum(halves, segment, num_segments=N_BAS * row_blocks + 1)[:-1]
        rounded = lax.optimization_barrier(partial_value.astype(jnp.bfloat16)).astype(jnp.float32)
        return jnp.sum(rounded.reshape(N_BAS, NBAS, width), axis=0).astype(jnp.bfloat16)

    grouped = lax.map(aux_block, jnp.arange(N_AUX, dtype=jnp.int32))
    transformed = grouped.transpose(1, 0, 2).reshape(NBAS, N_AUX * width)
    factor = 1.0 / (N_AUX * width)

    def exchange_rows(block):
        return lax.dot_general(block, transformed, (((1,), (1,)), ((), ())), preferred_element_type=jnp.float32) * factor

    result = lax.map(exchange_rows, transformed.reshape(N_AUX, NBAS // N_AUX, N_AUX * width))
    return result.reshape(NBAS, NBAS)
```

```python
import jax
import jax.numpy as jnp
from jax import lax
from jax.experimental import pallas as pl
from jax.experimental.pallas import tpu as pltpu
from jax.sharding import Mesh, PartitionSpec as P

NBAS = 20480
AUX_AXES = ("z", "y")
BAS_AXES = ("x", "core")
ALL_AXES = AUX_AXES + BAS_AXES
TILE_STEP = 32
COL_STEP = 256
SWAP = [(0, 1), (1, 0)]
VMEM_LIMIT = 56 * 1024 * 1024


def half_kernel(self_ref, owner_ref, col_ref, tiles_ref, orbital_ref, support_ref, out_ref, count_ref, kept_ref):
    step = pl.program_id(0)
    aux_here, tile_rows, tile_cols = tiles_ref.shape[1:]
    orbital_count = orbital_ref.shape[0]
    width = aux_here * orbital_count
    block_count = count_ref.shape[0]
    per_block = out_ref.shape[0] // block_count

    @pl.when(step == 0)
    def _():
        for block in range(block_count):
            count_ref[block] = 0
        orbital = lax.broadcasted_iota(jnp.int32, (orbital_count, width), 0)
        column = lax.broadcasted_iota(jnp.int32, (orbital_count, width), 1)
        spread = (lax.rem(column, orbital_count) == orbital).astype(jnp.float32)
        kept_ref[...] = lax.dot_general(
            (support_ref[...] == 1).astype(jnp.float32),
            spread,
            (((0,), (0,)), ((), ())),
            preferred_element_type=jnp.float32,
        )

    row = lax.bitwise_and(self_ref[0], 7)
    lane = lax.broadcasted_iota(jnp.int32, (tile_rows, width), 1)
    for index in range(tiles_ref.shape[0]):
        tile = step * tiles_ref.shape[0] + index
        block = lax.shift_right_logical(owner_ref[row, tile], 3)
        rank = count_ref[block]
        count_ref[block] = rank + 1
        col = col_ref[row, tile]
        chosen = orbital_ref[:, pl.ds(pl.multiple_of(col * tile_cols, tile_cols), tile_cols)]
        product = lax.dot_general(
            tiles_ref[index].reshape(aux_here * tile_rows, tile_cols),
            jnp.concatenate([chosen] * aux_here, axis=0),
            (((1,), (1,)), ((), ())),
            preferred_element_type=jnp.float32,
        )
        half = product[:tile_rows]
        for aux in range(1, aux_here):
            part = product[aux * tile_rows : (aux + 1) * tile_rows]
            half = jnp.where(lane >= aux * orbital_count, part, half)
        kept = kept_ref[pl.ds(col, 1), :] > 0.5
        out_ref[block * per_block + rank] = jnp.where(kept, half, 0.0).astype(out_ref.dtype)


def half_slots(myself, tiles, owners, cols, orbitals, support, block_count, per_block):
    count, aux_here, tile_rows, tile_cols = tiles.shape
    width = aux_here * orbitals.shape[0]
    index_spec = pl.BlockSpec((8, count), lambda i, self_ref: (self_ref[0] // 8, 0), memory_space=pltpu.SMEM)
    return pl.pallas_call(
        half_kernel,
        grid_spec=pltpu.PrefetchScalarGridSpec(
            num_scalar_prefetch=1,
            grid=(count // TILE_STEP,),
            in_specs=[
                index_spec,
                index_spec,
                pl.BlockSpec((TILE_STEP, aux_here, tile_rows, tile_cols), lambda i, _: (i, 0, 0, 0)),
                pl.BlockSpec(orbitals.shape, lambda i, _: (0, 0)),
                pl.BlockSpec(support.shape, lambda i, _: (0, 0)),
            ],
            out_specs=pl.BlockSpec((block_count * per_block, tile_rows, width), lambda i, _: (0, 0, 0)),
            scratch_shapes=[
                pltpu.SMEM((block_count,), jnp.int32),
                pltpu.VMEM((support.shape[1], width), jnp.float32),
            ],
        ),
        out_shape=jax.ShapeDtypeStruct((block_count * per_block, tile_rows, width), jnp.bfloat16),
        compiler_params=pltpu.CompilerParams(vmem_limit_bytes=VMEM_LIMIT),
        name="half_transform",
    )(myself, owners, cols, tiles, orbitals, support)


def sum_kernel(count_ref, list_ref, own_ref, other_ref, *refs):
    out_refs, total_ref = refs[:-1], refs[-1]
    total_ref[...] = jnp.zeros_like(total_ref)
    for side, slots_ref in enumerate((own_ref, other_ref)):

        def add(index, carry, side=side, slots_ref=slots_ref):
            entry = list_ref[side, index]
            slot = lax.shift_right_logical(entry, 9)
            place = lax.bitwise_and(entry, 511)
            total_ref[place] += slots_ref[slot].astype(jnp.float32)
            return carry

        lax.fori_loop(0, count_ref[side], add, 0)
    first = 0
    for out_ref in out_refs:
        blocks = out_ref.shape[0]
        out_ref[...] = total_ref[pl.ds(first, blocks)].astype(out_ref.dtype)
        first += blocks


def sum_slots(counts, entries, own, other, part):
    tile_shape = own.shape[1:]
    sizes = [part] + [part // 2] * 6
    places = 4 * part
    outs = pl.pallas_call(
        sum_kernel,
        in_specs=[
            pl.BlockSpec(memory_space=pltpu.SMEM),
            pl.BlockSpec(memory_space=pltpu.SMEM),
            pl.BlockSpec(memory_space=pltpu.VMEM),
            pl.BlockSpec(memory_space=pltpu.VMEM),
        ],
        out_specs=[pl.BlockSpec(memory_space=pltpu.VMEM)] * len(sizes),
        out_shape=[jax.ShapeDtypeStruct((size,) + tile_shape, jnp.bfloat16) for size in sizes],
        scratch_shapes=[pltpu.VMEM((places,) + tile_shape, jnp.float32)],
        compiler_params=pltpu.CompilerParams(vmem_limit_bytes=VMEM_LIMIT),
        name="sum_slots",
    )(counts, entries, own, other)
    return outs


def slot_entries(owners, rows, block, x_place, core, slots_per_source, rows_per_part):
    sides, sources, tiles_here = owners.shape
    hit = lax.shift_right_logical(owners, 3) == block
    mine = jnp.logical_and(hit, (rows // rows_per_part) % 2 == core)
    before = jnp.triu(jnp.ones((tiles_here, tiles_here), jnp.bfloat16), 1)
    flags = jnp.stack([hit, mine]).astype(jnp.bfloat16)
    ahead = jnp.einsum("fkst,tu->fksu", flags, before, preferred_element_type=jnp.float32).astype(jnp.int32)
    slot = jnp.arange(sources, dtype=jnp.int32)[None, :, None] * slots_per_source + ahead[0]
    part = (rows // (2 * rows_per_part) - x_place) & 3
    place = part * rows_per_part + rows % rows_per_part
    mine_counts = jnp.sum(mine.astype(jnp.int32), axis=2)
    earlier = jnp.cumsum(mine_counts, axis=1) - mine_counts
    position = jnp.where(mine, ahead[1] + earlier[:, :, None], -1).reshape(sides, 1, sources * tiles_here)
    packed = (slot * 512 + place).reshape(sides, 1, sources * tiles_here)
    wanted = jnp.arange(sources * slots_per_source, dtype=jnp.int32)[None, :, None]
    entries = jnp.sum(jnp.where(position == wanted, packed, 0), axis=2)
    return jnp.sum(mine_counts, axis=1), entries


def shift(value, axis, by):
    return lax.ppermute(value, axis, [(i, (i + by) % 4) for i in range(4)])


def reduce_over_x(own, p1a, p1b, p2a, p2b, p3a, p3b):
    def add(*values):
        total = sum(value.astype(jnp.float32) for value in values).astype(jnp.bfloat16)
        return total.reshape(-1, total.shape[-1])

    far_a, far_b = shift(p2a, "x", 1), shift(p2b, "x", -1)
    low_b, high_a = shift(p1b, "x", 1), shift(p3a, "x", -1)
    low_a = shift(add(p1a, far_a).reshape(p1a.shape), "x", 1)
    high_b = shift(add(p3b, far_b).reshape(p3b.shape), "x", -1)
    low, high = jnp.concatenate([low_a, low_b]), jnp.concatenate([high_a, high_b])
    return add(own, low, high)


def device(z, y, x, core):
    return ((z * 4 + y) * 4 + x) * 2 + core


def shift_turned(value, second, by):
    pairs = []
    for z in range(4):
        for y in range(4):
            for x in range(4):
                for core in range(2):
                    along_z = (core == 0) != second
                    to_z, to_y = ((z + by) % 4, y) if along_z else (z, (y + by) % 4)
                    pairs.append((device(z, y, x, core), device(to_z, to_y, x, core)))
    return lax.ppermute(value, ALL_AXES, pairs)


def spread_pairs(turn):
    along_x, along_zy = [], []
    for zg in range(4):
        for yg in range(4):
            for z in range(4):
                for high in range(2):
                    y = 2 * high + (yg // 2 ^ turn)
                    x = (zg + y + z) % 4
                    along_x.append((device(zg, yg, z, high), device(zg, yg, x, high)))
                    along_zy.append((device(zg, yg, x, high), device(z, y, x, yg % 2)))
    return along_x, along_zy


def gather_both(local):
    stage = lax.optimization_barrier
    middle = local.shape[0] // 2
    turned = lax.axis_index("y") // 2 == 1
    halves = local[:middle], local[middle:]
    pairs = [spread_pairs(turn) for turn in range(2)]

    low, high = shift_turned(local, False, 1), shift_turned(local, False, -1)
    rows = [lax.ppermute(jnp.where(turned, halves[1 - t], halves[t]), ALL_AXES, pairs[t][0]) for t in range(2)]
    low, high, rows = stage((low, high, rows))

    far_a, far_b = shift_turned(high[:middle], False, -1), shift_turned(low[middle:], False, 1)
    rows = [lax.ppermute(rows[t], ALL_AXES, pairs[t][1]) for t in range(2)]
    near = jnp.stack([local, low])
    far = jnp.stack([high, jnp.concatenate([far_a, far_b])])
    rows = jnp.stack(rows)
    near, far, rows = stage((near, far, rows))

    near_low, near_high = shift_turned(near, True, 1), shift_turned(near, True, -1)
    rows_low, rows_high = shift(rows, "x", 1), shift(rows, "x", -1)
    far, near_low, near_high, rows_low, rows_high = stage((far, near_low, near_high, rows_low, rows_high))

    far_low, far_high = shift_turned(far, True, 1), shift_turned(far, True, -1)
    rows_far = jnp.stack([shift(rows_high[0], "x", -1), shift(rows_low[1], "x", 1)])
    near_high, far_low, far_high, rows_far = stage((near_high, far_low, far_high, rows_far))

    near_far, far_far = shift_turned(near_high, True, -1), shift_turned(far_low, True, 1)
    rows_near, rows_far = jnp.stack([rows, rows_low]), jnp.stack([rows_high, rows_far])
    rows = [rows_near, rows_far, lax.ppermute(rows_near, "core", SWAP), lax.ppermute(rows_far, "core", SWAP)]
    return [near, far, near_low, far_low, near_high, far_high, near_far, far_far], rows


def exchange_kernel(at_ref, *refs, factor):
    row_refs, col_refs, (out_ref, row_data) = refs[:4], refs[4:-2], refs[-2:]
    width = row_refs[0].shape[-1]

    @pl.when(pl.program_id(0) == 0)
    def _():
        z_place, y_place, x_place, core = (at_ref[i] for i in range(4))

        def order(offset):
            odd = lax.bitwise_and(offset, 1)
            half = lax.shift_right_logical(offset, 1)
            return jnp.where(odd == 1, 2 - half, offset + half)

        for core_from, pair in ((core, row_refs[:2]), (1 - core, row_refs[2:])):
            for index, offset in enumerate((0, -1, 1, 2)):
                for turn in range(2):
                    zg = lax.bitwise_and(x_place + offset - y_place - z_place, 3)
                    yg = 2 * lax.bitwise_xor(lax.bitwise_and(y_place, 1), turn) + core_from
                    z_at = order(lax.bitwise_and(zg - z_place, 3))
                    y_at = order(lax.bitwise_and(yg - y_place, 3))
                    place = jnp.where(core == 0, 4 * y_at + z_at, 4 * z_at + y_at)
                    columns = pl.ds(pl.multiple_of(place * width, width), width)
                    row_data[:, columns] = pair[index // 2][index % 2, turn]

    columns = jnp.concatenate([col_ref[i] for col_ref in col_refs for i in range(2)], axis=1)
    out_ref[...] = (
        lax.dot_general(
            row_data[...], columns, (((1,), (1,)), ((), ())), preferred_element_type=jnp.float32
        )
        * factor
    )


def exchange_block(at, row_parts, pieces):
    offsets, turns, rows, width = row_parts[0].shape
    col_count = pieces[0].shape[1]
    depth = 2 * len(pieces) * width
    return pl.pallas_call(
        lambda *refs: exchange_kernel(*refs, factor=1.0 / depth),
        grid=(col_count // COL_STEP,),
        in_specs=[pl.BlockSpec(memory_space=pltpu.SMEM)]
        + [pl.BlockSpec(row_parts[0].shape, lambda j: (0, 0, 0, 0))] * len(row_parts)
        + [pl.BlockSpec((2, COL_STEP, width), lambda j: (0, j, 0))] * len(pieces),
        out_specs=pl.BlockSpec((rows, COL_STEP), lambda j: (0, j)),
        out_shape=jax.ShapeDtypeStruct((rows, col_count), jnp.float32),
        scratch_shapes=[pltpu.VMEM((rows, depth), jnp.bfloat16)],
        compiler_params=pltpu.CompilerParams(vmem_limit_bytes=VMEM_LIMIT),
        name="exchange",
    )(at, *row_parts, *pieces)


def shards(tiles, tile_owner, pair_rows, pair_cols, orbitals, support):
    tiles_here, _, tile_rows, _ = tiles.shape
    aux_count = lax.axis_size(AUX_AXES)
    bas_count = lax.axis_size(BAS_AXES)
    x_count = lax.axis_size("x")
    block = lax.axis_index(AUX_AXES)
    at = [lax.axis_index(axis) for axis in ALL_AXES]
    x_place, core = at[2:]
    myself = block * bas_count + lax.axis_index(BAS_AXES)
    slots_per_source = 2 * bas_count
    rows_per_part = NBAS // tile_rows // bas_count

    owner_flat = tile_owner[:, 0]
    by_device = (aux_count * bas_count, tiles_here)
    outgoing = half_slots(
        myself[None].astype(jnp.int32),
        tiles,
        owner_flat.reshape(by_device),
        pair_cols.reshape(by_device),
        orbitals,
        support,
        aux_count,
        slots_per_source,
    )
    own = lax.all_to_all(outgoing, AUX_AXES, split_axis=0, concat_axis=0, tiled=True)

    def sources(flat):
        near = lax.dynamic_index_in_dim(flat.reshape(aux_count, x_count, 2, tiles_here), x_place, 1, keepdims=False)
        return jnp.where(core == 0, near, near[:, ::-1]).transpose(1, 0, 2)

    counts, entries = slot_entries(
        sources(owner_flat), sources(pair_rows), block, x_place, core, slots_per_source, rows_per_part
    )
    other = lax.ppermute(own, "core", SWAP)
    local = reduce_over_x(*sum_slots(counts, entries, own, other, rows_per_part))
    pieces, row_parts = gather_both(local)
    return exchange_block(jnp.stack(at).astype(jnp.int32), row_parts, pieces)


def solution(mesh):
    fine = Mesh(mesh.devices.reshape(4, 4, 4, 2), ALL_AXES)
    in_specs = (P(ALL_AXES, None, None, None), P(), P(), P(), P(), P())
    out_specs = P(AUX_AXES, BAS_AXES)
    return jax.shard_map(shards, mesh=fine, in_specs=in_specs, out_specs=out_specs, check_vma=False)
```

```python
import jax
import jax.numpy as jnp
from jax import lax
from jax.experimental import pallas as pl
from jax.experimental.pallas import tpu as pltpu
from jax.sharding import Mesh, PartitionSpec as P

NBAS = 20480
AUX_AXES = ("z", "y")
BAS_AXES = ("x", "core")
ALL_AXES = AUX_AXES + BAS_AXES
TILE_STEP = 32
COL_STEP = 256
SWAP = [(0, 1), (1, 0)]
VMEM_LIMIT = 56 * 1024 * 1024


def half_kernel(self_ref, owner_ref, col_ref, tiles_ref, orbital_ref, support_ref, out_ref, count_ref, kept_ref):
    step = pl.program_id(0)
    aux_here, tile_rows, tile_cols = tiles_ref.shape[1:]
    orbital_count = orbital_ref.shape[0]
    width = aux_here * orbital_count
    block_count = count_ref.shape[0]
    per_block = out_ref.shape[0] // block_count

    @pl.when(step == 0)
    def _():
        for block in range(block_count):
            count_ref[block] = 0
        orbital = lax.broadcasted_iota(jnp.int32, (orbital_count, width), 0)
        column = lax.broadcasted_iota(jnp.int32, (orbital_count, width), 1)
        spread = (lax.rem(column, orbital_count) == orbital).astype(jnp.float32)
        kept_ref[...] = lax.dot_general(
            (support_ref[...] == 1).astype(jnp.float32),
            spread,
            (((0,), (0,)), ((), ())),
            preferred_element_type=jnp.float32,
        )

    row = lax.bitwise_and(self_ref[0], 7)
    lane = lax.broadcasted_iota(jnp.int32, (tile_rows, width), 1)
    for index in range(tiles_ref.shape[0]):
        tile = step * tiles_ref.shape[0] + index
        block = lax.shift_right_logical(owner_ref[row, tile], 3)
        rank = count_ref[block]
        count_ref[block] = rank + 1
        col = col_ref[row, tile]
        chosen = orbital_ref[:, pl.ds(pl.multiple_of(col * tile_cols, tile_cols), tile_cols)]
        product = lax.dot_general(
            tiles_ref[index].reshape(aux_here * tile_rows, tile_cols),
            jnp.concatenate([chosen] * aux_here, axis=0),
            (((1,), (1,)), ((), ())),
            preferred_element_type=jnp.float32,
        )
        half = product[:tile_rows]
        for aux in range(1, aux_here):
            part = product[aux * tile_rows : (aux + 1) * tile_rows]
            half = jnp.where(lane >= aux * orbital_count, part, half)
        kept = kept_ref[pl.ds(col, 1), :] > 0.5
        out_ref[block * per_block + rank] = jnp.where(kept, half, 0.0).astype(out_ref.dtype)


def half_slots(myself, tiles, owners, cols, orbitals, support, block_count, per_block):
    count, aux_here, tile_rows, tile_cols = tiles.shape
    width = aux_here * orbitals.shape[0]
    index_spec = pl.BlockSpec((8, count), lambda i, self_ref: (self_ref[0] // 8, 0), memory_space=pltpu.SMEM)
    return pl.pallas_call(
        half_kernel,
        grid_spec=pltpu.PrefetchScalarGridSpec(
            num_scalar_prefetch=1,
            grid=(count // TILE_STEP,),
            in_specs=[
                index_spec,
                index_spec,
                pl.BlockSpec((TILE_STEP, aux_here, tile_rows, tile_cols), lambda i, _: (i, 0, 0, 0)),
                pl.BlockSpec(orbitals.shape, lambda i, _: (0, 0)),
                pl.BlockSpec(support.shape, lambda i, _: (0, 0)),
            ],
            out_specs=pl.BlockSpec((block_count * per_block, tile_rows, width), lambda i, _: (0, 0, 0)),
            scratch_shapes=[
                pltpu.SMEM((block_count,), jnp.int32),
                pltpu.VMEM((support.shape[1], width), jnp.float32),
            ],
        ),
        out_shape=jax.ShapeDtypeStruct((block_count * per_block, tile_rows, width), jnp.bfloat16),
        compiler_params=pltpu.CompilerParams(vmem_limit_bytes=VMEM_LIMIT),
        name="half_transform",
    )(myself, owners, cols, tiles, orbitals, support)


def sum_kernel(count_ref, list_ref, own_ref, other_ref, *refs):
    out_refs, total_ref = refs[:-1], refs[-1]
    total_ref[...] = jnp.zeros_like(total_ref)
    for side, slots_ref in enumerate((own_ref, other_ref)):

        def add(index, carry, side=side, slots_ref=slots_ref):
            entry = list_ref[side, index]
            slot = lax.shift_right_logical(entry, 9)
            place = lax.bitwise_and(entry, 511)
            total_ref[place] += slots_ref[slot].astype(jnp.float32)
            return carry

        lax.fori_loop(0, count_ref[side], add, 0)
    first = 0
    for out_ref in out_refs:
        blocks = out_ref.shape[0]
        out_ref[...] = total_ref[pl.ds(first, blocks)].astype(out_ref.dtype)
        first += blocks


def sum_slots(counts, entries, own, other, part):
    tile_shape = own.shape[1:]
    sizes = [part] + [part // 2] * 6
    places = 4 * part
    outs = pl.pallas_call(
        sum_kernel,
        in_specs=[
            pl.BlockSpec(memory_space=pltpu.SMEM),
            pl.BlockSpec(memory_space=pltpu.SMEM),
            pl.BlockSpec(memory_space=pltpu.VMEM),
            pl.BlockSpec(memory_space=pltpu.VMEM),
        ],
        out_specs=[pl.BlockSpec(memory_space=pltpu.VMEM)] * len(sizes),
        out_shape=[jax.ShapeDtypeStruct((size,) + tile_shape, jnp.bfloat16) for size in sizes],
        scratch_shapes=[pltpu.VMEM((places,) + tile_shape, jnp.float32)],
        compiler_params=pltpu.CompilerParams(vmem_limit_bytes=VMEM_LIMIT),
        name="sum_slots",
    )(counts, entries, own, other)
    return outs


def slot_entries(owners, rows, block, x_place, core, slots_per_source, rows_per_part):
    sides, sources, tiles_here = owners.shape
    hit = lax.shift_right_logical(owners, 3) == block
    mine = jnp.logical_and(hit, (rows // rows_per_part) % 2 == core)
    before = jnp.triu(jnp.ones((tiles_here, tiles_here), jnp.bfloat16), 1)
    flags = jnp.stack([hit, mine]).astype(jnp.bfloat16)
    ahead = jnp.einsum("fkst,tu->fksu", flags, before, preferred_element_type=jnp.float32).astype(jnp.int32)
    slot = jnp.arange(sources, dtype=jnp.int32)[None, :, None] * slots_per_source + ahead[0]
    part = (rows // (2 * rows_per_part) - x_place) & 3
    place = part * rows_per_part + rows % rows_per_part
    mine_counts = jnp.sum(mine.astype(jnp.int32), axis=2)
    earlier = jnp.cumsum(mine_counts, axis=1) - mine_counts
    position = jnp.where(mine, ahead[1] + earlier[:, :, None], -1).reshape(sides, 1, sources * tiles_here)
    packed = (slot * 512 + place).reshape(sides, 1, sources * tiles_here)
    wanted = jnp.arange(sources * slots_per_source, dtype=jnp.int32)[None, :, None]
    entries = jnp.sum(jnp.where(position == wanted, packed, 0), axis=2)
    return jnp.sum(mine_counts, axis=1), entries


def shift(value, axis, by):
    return lax.ppermute(value, axis, [(i, (i + by) % 4) for i in range(4)])


def reduce_over_x(own, p1a, p1b, p2a, p2b, p3a, p3b):
    def add(*values):
        total = sum(value.astype(jnp.float32) for value in values).astype(jnp.bfloat16)
        return total.reshape(-1, total.shape[-1])

    far_a, far_b = shift(p2a, "x", 1), shift(p2b, "x", -1)
    low_b, high_a = shift(p1b, "x", 1), shift(p3a, "x", -1)
    low_a = shift(add(p1a, far_a).reshape(p1a.shape), "x", 1)
    high_b = shift(add(p3b, far_b).reshape(p3b.shape), "x", -1)
    low, high = jnp.concatenate([low_a, low_b]), jnp.concatenate([high_a, high_b])
    return add(own, low, high)


def device(z, y, x, core):
    return ((z * 4 + y) * 4 + x) * 2 + core


def shift_turned(value, second, by):
    pairs = []
    for z in range(4):
        for y in range(4):
            for x in range(4):
                for core in range(2):
                    along_z = (core == 0) != second
                    to_z, to_y = ((z + by) % 4, y) if along_z else (z, (y + by) % 4)
                    pairs.append((device(z, y, x, core), device(to_z, to_y, x, core)))
    return lax.ppermute(value, ALL_AXES, pairs)


def spread_pairs(turn):
    along_x, along_zy = [], []
    for zg in range(4):
        for yg in range(4):
            for z in range(4):
                for high in range(2):
                    y = 2 * high + (yg // 2 ^ turn)
                    x = (zg + y + z) % 4
                    along_x.append((device(zg, yg, z, high), device(zg, yg, x, high)))
                    along_zy.append((device(zg, yg, x, high), device(z, y, x, yg % 2)))
    return along_x, along_zy


def gather_both(local):
    stage = lax.optimization_barrier
    middle = local.shape[0] // 2
    turned = lax.axis_index("y") // 2 == 1
    halves = local[:middle], local[middle:]
    pairs = [spread_pairs(turn) for turn in range(2)]

    low, high = shift_turned(local, False, 1), shift_turned(local, False, -1)
    rows = [lax.ppermute(jnp.where(turned, halves[1 - t], halves[t]), ALL_AXES, pairs[t][0]) for t in range(2)]
    low, high, rows = stage((low, high, rows))

    far_a, far_b = shift_turned(high[:middle], False, -1), shift_turned(low[middle:], False, 1)
    rows = [lax.ppermute(rows[t], ALL_AXES, pairs[t][1]) for t in range(2)]
    near = jnp.stack([local, low])
    near_low, near_high = shift_turned(near, True, 1), shift_turned(near, True, -1)
    far = jnp.stack([high, jnp.concatenate([far_a, far_b])])
    rows = jnp.stack(rows)
    far, rows = stage((far, rows))

    rows_low, rows_high = shift(rows, "x", 1), shift(rows, "x", -1)
    far_low, far_high = shift_turned(far, True, 1), shift_turned(far, True, -1)
    rows_far = jnp.stack([shift(rows_high[0], "x", -1), shift(rows_low[1], "x", 1)])
    near_far, far_far = shift_turned(near_high, True, -1), shift_turned(far_low, True, 1)
    rows_near, rows_far = jnp.stack([rows, rows_low]), jnp.stack([rows_high, rows_far])
    rows = [rows_near, rows_far, lax.ppermute(rows_near, "core", SWAP), lax.ppermute(rows_far, "core", SWAP)]
    return [near, far, near_low, far_low, near_high, far_high, near_far, far_far], rows


def exchange_kernel(at_ref, *refs, factor):
    row_refs, col_refs, (out_ref, row_data) = refs[:4], refs[4:-2], refs[-2:]
    width = row_refs[0].shape[-1]

    @pl.when(pl.program_id(0) == 0)
    def _():
        z_place, y_place, x_place, core = (at_ref[i] for i in range(4))

        def order(offset):
            odd = lax.bitwise_and(offset, 1)
            half = lax.shift_right_logical(offset, 1)
            return jnp.where(odd == 1, 2 - half, offset + half)

        for core_from, pair in ((core, row_refs[:2]), (1 - core, row_refs[2:])):
            for index, offset in enumerate((0, -1, 1, 2)):
                for turn in range(2):
                    zg = lax.bitwise_and(x_place + offset - y_place - z_place, 3)
                    yg = 2 * lax.bitwise_xor(lax.bitwise_and(y_place, 1), turn) + core_from
                    z_at = order(lax.bitwise_and(zg - z_place, 3))
                    y_at = order(lax.bitwise_and(yg - y_place, 3))
                    place = jnp.where(core == 0, 4 * y_at + z_at, 4 * z_at + y_at)
                    columns = pl.ds(pl.multiple_of(place * width, width), width)
                    row_data[:, columns] = pair[index // 2][index % 2, turn]

    columns = jnp.concatenate([col_ref[i] for col_ref in col_refs for i in range(2)], axis=1)
    out_ref[...] = (
        lax.dot_general(
            row_data[...], columns, (((1,), (1,)), ((), ())), preferred_element_type=jnp.float32
        )
        * factor
    )


def exchange_block(at, row_parts, pieces):
    offsets, turns, rows, width = row_parts[0].shape
    col_count = pieces[0].shape[1]
    depth = 2 * len(pieces) * width
    return pl.pallas_call(
        lambda *refs: exchange_kernel(*refs, factor=1.0 / depth),
        grid=(col_count // COL_STEP,),
        in_specs=[pl.BlockSpec(memory_space=pltpu.SMEM)]
        + [pl.BlockSpec(row_parts[0].shape, lambda j: (0, 0, 0, 0))] * len(row_parts)
        + [pl.BlockSpec((2, COL_STEP, width), lambda j: (0, j, 0))] * len(pieces),
        out_specs=pl.BlockSpec((rows, COL_STEP), lambda j: (0, j)),
        out_shape=jax.ShapeDtypeStruct((rows, col_count), jnp.float32),
        scratch_shapes=[pltpu.VMEM((rows, depth), jnp.bfloat16)],
        compiler_params=pltpu.CompilerParams(vmem_limit_bytes=VMEM_LIMIT),
        name="exchange",
    )(at, *row_parts, *pieces)


def shards(tiles, tile_owner, pair_rows, pair_cols, orbitals, support):
    tiles_here, _, tile_rows, _ = tiles.shape
    aux_count = lax.axis_size(AUX_AXES)
    bas_count = lax.axis_size(BAS_AXES)
    x_count = lax.axis_size("x")
    block = lax.axis_index(AUX_AXES)
    at = [lax.axis_index(axis) for axis in ALL_AXES]
    x_place, core = at[2:]
    myself = block * bas_count + lax.axis_index(BAS_AXES)
    slots_per_source = 2 * bas_count
    rows_per_part = NBAS // tile_rows // bas_count

    owner_flat = tile_owner[:, 0]
    by_device = (aux_count * bas_count, tiles_here)
    outgoing = half_slots(
        myself[None].astype(jnp.int32),
        tiles,
        owner_flat.reshape(by_device),
        pair_cols.reshape(by_device),
        orbitals,
        support,
        aux_count,
        slots_per_source,
    )
    own = lax.all_to_all(outgoing, AUX_AXES, split_axis=0, concat_axis=0, tiled=True)

    def sources(flat):
        near = lax.dynamic_index_in_dim(flat.reshape(aux_count, x_count, 2, tiles_here), x_place, 1, keepdims=False)
        return jnp.where(core == 0, near, near[:, ::-1]).transpose(1, 0, 2)

    counts, entries = slot_entries(
        sources(owner_flat), sources(pair_rows), block, x_place, core, slots_per_source, rows_per_part
    )
    other = lax.ppermute(own, "core", SWAP)
    local = reduce_over_x(*sum_slots(counts, entries, own, other, rows_per_part))
    pieces, row_parts = gather_both(local)
    return exchange_block(jnp.stack(at).astype(jnp.int32), row_parts, pieces)


def solution(mesh):
    fine = Mesh(mesh.devices.reshape(4, 4, 4, 2), ALL_AXES)
    in_specs = (P(ALL_AXES, None, None, None), P(), P(), P(), P(), P())
    out_specs = P(AUX_AXES, BAS_AXES)
    return jax.shard_map(shards, mesh=fine, in_specs=in_specs, out_specs=out_specs, check_vma=False)
```

```python
import jax
import jax.numpy as jnp
from jax import lax
from jax.experimental import pallas as pl
from jax.experimental.pallas import tpu as pltpu
from jax.sharding import Mesh, PartitionSpec as P

NBAS = 20480
AUX_AXES = ("z", "y")
BAS_AXES = ("x", "core")
ALL_AXES = AUX_AXES + BAS_AXES
TILE_STEP = 32
COL_STEP = 256
COL_LOAD = 512
OUT_PARTS = 4
SWAP = [(0, 1), (1, 0)]
VMEM_LIMIT = 56 * 1024 * 1024
EXCHANGE_LIMIT = 36 * 1024 * 1024


def half_kernel(self_ref, owner_ref, col_ref, tiles_ref, orbital_ref, support_ref, out_ref, count_ref, kept_ref):
    step = pl.program_id(0)
    aux_here, tile_rows, tile_cols = tiles_ref.shape[1:]
    orbital_count = orbital_ref.shape[0]
    width = aux_here * orbital_count
    block_count = count_ref.shape[0]
    per_block = out_ref.shape[0] // block_count

    @pl.when(step == 0)
    def _():
        for block in range(block_count):
            count_ref[block] = 0
        orbital = lax.broadcasted_iota(jnp.int32, (orbital_count, width), 0)
        column = lax.broadcasted_iota(jnp.int32, (orbital_count, width), 1)
        spread = (lax.rem(column, orbital_count) == orbital).astype(jnp.float32)
        kept_ref[...] = lax.dot_general(
            (support_ref[...] == 1).astype(jnp.float32),
            spread,
            (((0,), (0,)), ((), ())),
            preferred_element_type=jnp.float32,
        )

    row = lax.bitwise_and(self_ref[0], 7)
    lane = lax.broadcasted_iota(jnp.int32, (tile_rows, width), 1)
    for index in range(tiles_ref.shape[0]):
        tile = step * tiles_ref.shape[0] + index
        block = lax.shift_right_logical(owner_ref[row, tile], 3)
        rank = count_ref[block]
        count_ref[block] = rank + 1
        col = col_ref[row, tile]
        chosen = orbital_ref[:, pl.ds(pl.multiple_of(col * tile_cols, tile_cols), tile_cols)]
        product = lax.dot_general(
            tiles_ref[index].reshape(aux_here * tile_rows, tile_cols),
            jnp.concatenate([chosen] * aux_here, axis=0),
            (((1,), (1,)), ((), ())),
            preferred_element_type=jnp.float32,
        )
        half = product[:tile_rows]
        for aux in range(1, aux_here):
            part = product[aux * tile_rows : (aux + 1) * tile_rows]
            half = jnp.where(lane >= aux * orbital_count, part, half)
        kept = kept_ref[pl.ds(col, 1), :] > 0.5
        out_ref[block * per_block + rank] = jnp.where(kept, half, 0.0).astype(out_ref.dtype)


def half_slots(myself, tiles, owners, cols, orbitals, support, block_count, per_block):
    count, aux_here, tile_rows, tile_cols = tiles.shape
    width = aux_here * orbitals.shape[0]
    index_spec = pl.BlockSpec((8, count), lambda i, self_ref: (self_ref[0] // 8, 0), memory_space=pltpu.SMEM)
    return pl.pallas_call(
        half_kernel,
        grid_spec=pltpu.PrefetchScalarGridSpec(
            num_scalar_prefetch=1,
            grid=(count // TILE_STEP,),
            in_specs=[
                index_spec,
                index_spec,
                pl.BlockSpec((TILE_STEP, aux_here, tile_rows, tile_cols), lambda i, _: (i, 0, 0, 0)),
                pl.BlockSpec(orbitals.shape, lambda i, _: (0, 0)),
                pl.BlockSpec(support.shape, lambda i, _: (0, 0)),
            ],
            out_specs=pl.BlockSpec((block_count * per_block, tile_rows, width), lambda i, _: (0, 0, 0)),
            scratch_shapes=[
                pltpu.SMEM((block_count,), jnp.int32),
                pltpu.VMEM((support.shape[1], width), jnp.float32),
            ],
        ),
        out_shape=jax.ShapeDtypeStruct((block_count * per_block, tile_rows, width), jnp.bfloat16),
        compiler_params=pltpu.CompilerParams(vmem_limit_bytes=VMEM_LIMIT),
        name="half_transform",
    )(myself, owners, cols, tiles, orbitals, support)


def sum_kernel(count_ref, list_ref, own_ref, other_ref, *refs):
    out_refs, total_ref = refs[:-1], refs[-1]
    total_ref[...] = jnp.zeros_like(total_ref)
    for side, slots_ref in enumerate((own_ref, other_ref)):

        def add(index, carry, side=side, slots_ref=slots_ref):
            entry = list_ref[side, index]
            slot = lax.shift_right_logical(entry, 9)
            place = lax.bitwise_and(entry, 511)
            total_ref[place] += slots_ref[slot].astype(jnp.float32)
            return carry

        lax.fori_loop(0, count_ref[side], add, 0)
    first = 0
    for out_ref in out_refs:
        blocks = out_ref.shape[0]
        out_ref[...] = total_ref[pl.ds(first, blocks)].astype(out_ref.dtype)
        first += blocks


def sum_slots(counts, entries, own, other, part):
    tile_shape = own.shape[1:]
    sizes = [part] + [part // 2] * 6
    places = 4 * part
    outs = pl.pallas_call(
        sum_kernel,
        in_specs=[
            pl.BlockSpec(memory_space=pltpu.SMEM),
            pl.BlockSpec(memory_space=pltpu.SMEM),
            pl.BlockSpec(memory_space=pltpu.VMEM),
            pl.BlockSpec(memory_space=pltpu.VMEM),
        ],
        out_specs=[pl.BlockSpec(memory_space=pltpu.VMEM)] * len(sizes),
        out_shape=[jax.ShapeDtypeStruct((size,) + tile_shape, jnp.bfloat16) for size in sizes],
        scratch_shapes=[pltpu.VMEM((places,) + tile_shape, jnp.float32)],
        compiler_params=pltpu.CompilerParams(vmem_limit_bytes=VMEM_LIMIT),
        name="sum_slots",
    )(counts, entries, own, other)
    return outs


def slot_entries(owners, rows, block, x_place, core, slots_per_source, rows_per_part):
    sides, sources, tiles_here = owners.shape
    hit = lax.shift_right_logical(owners, 3) == block
    mine = jnp.logical_and(hit, (rows // rows_per_part) % 2 == core)
    before = jnp.triu(jnp.ones((tiles_here, tiles_here), jnp.bfloat16), 1)
    flags = jnp.stack([hit, mine]).astype(jnp.bfloat16)
    ahead = jnp.einsum("fkst,tu->fksu", flags, before, preferred_element_type=jnp.float32).astype(jnp.int32)
    slot = jnp.arange(sources, dtype=jnp.int32)[None, :, None] * slots_per_source + ahead[0]
    part = (rows // (2 * rows_per_part) - x_place) & 3
    place = part * rows_per_part + rows % rows_per_part
    mine_counts = jnp.sum(mine.astype(jnp.int32), axis=2)
    earlier = jnp.cumsum(mine_counts, axis=1) - mine_counts
    position = jnp.where(mine, ahead[1] + earlier[:, :, None], -1).reshape(sides, 1, sources * tiles_here)
    packed = (slot * 512 + place).reshape(sides, 1, sources * tiles_here)
    wanted = jnp.arange(sources * slots_per_source, dtype=jnp.int32)[None, :, None]
    entries = jnp.sum(jnp.where(position == wanted, packed, 0), axis=2)
    return jnp.sum(mine_counts, axis=1), entries


def shift(value, axis, by):
    return lax.ppermute(value, axis, [(i, (i + by) % 4) for i in range(4)])


def reduce_over_x(own, p1a, p1b, p2a, p2b, p3a, p3b):
    def add(*values):
        total = sum(value.astype(jnp.float32) for value in values).astype(jnp.bfloat16)
        return total.reshape(-1, total.shape[-1])

    far_a, far_b = shift(p2a, "x", 1), shift(p2b, "x", -1)
    low_b, high_a = shift(p1b, "x", 1), shift(p3a, "x", -1)
    low_a = shift(add(p1a, far_a).reshape(p1a.shape), "x", 1)
    high_b = shift(add(p3b, far_b).reshape(p3b.shape), "x", -1)
    low, high = jnp.concatenate([low_a, low_b]), jnp.concatenate([high_a, high_b])
    return add(own, low, high)


def device(z, y, x, core):
    return ((z * 4 + y) * 4 + x) * 2 + core


def shift_turned(value, second, by):
    pairs = []
    for z in range(4):
        for y in range(4):
            for x in range(4):
                for core in range(2):
                    along_z = (core == 0) != second
                    to_z, to_y = ((z + by) % 4, y) if along_z else (z, (y + by) % 4)
                    pairs.append((device(z, y, x, core), device(to_z, to_y, x, core)))
    return lax.ppermute(value, ALL_AXES, pairs)


def spread_pairs(turn):
    along_x, along_zy = [], []
    for zg in range(4):
        for yg in range(4):
            for z in range(4):
                for high in range(2):
                    y = 2 * high + (yg // 2 ^ turn)
                    x = (zg + y + z) % 4
                    along_x.append((device(zg, yg, z, high), device(zg, yg, x, high)))
                    along_zy.append((device(zg, yg, x, high), device(z, y, x, yg % 2)))
    return along_x, along_zy


def gather_both(local):
    stage = lax.optimization_barrier
    middle = local.shape[0] // 2
    turned = lax.axis_index("y") // 2 == 1
    halves = local[:middle], local[middle:]
    pairs = [spread_pairs(turn) for turn in range(2)]

    low, high = shift_turned(local, False, 1), shift_turned(local, False, -1)
    rows = [lax.ppermute(jnp.where(turned, halves[1 - t], halves[t]), ALL_AXES, pairs[t][0]) for t in range(2)]
    low, high, rows = stage((low, high, rows))

    far_a, far_b = shift_turned(high[:middle], False, -1), shift_turned(low[middle:], False, 1)
    rows = [lax.ppermute(rows[t], ALL_AXES, pairs[t][1]) for t in range(2)]
    near = jnp.stack([local, low])
    near_low, near_high = shift_turned(near, True, 1), shift_turned(near, True, -1)
    far = jnp.stack([high, jnp.concatenate([far_a, far_b])])
    rows = jnp.stack(rows)
    far, rows = stage((far, rows))

    rows_low, rows_high = shift(rows, "x", 1), shift(rows, "x", -1)
    far_low, far_high = shift_turned(far, True, 1), shift_turned(far, True, -1)
    rows_far = jnp.stack([shift(rows_high[0], "x", -1), shift(rows_low[1], "x", 1)])
    near_far, far_far = shift_turned(near_high, True, -1), shift_turned(far_low, True, 1)
    rows_near, rows_far = jnp.stack([rows, rows_low]), jnp.stack([rows_high, rows_far])
    rows = [rows_near, rows_far, lax.ppermute(rows_near, "core", SWAP), lax.ppermute(rows_far, "core", SWAP)]
    return [near, far, near_low, far_low, near_high, far_high, near_far, far_far], rows


def exchange_kernel(at_ref, *refs, factor):
    row_refs, col_refs = refs[:4], refs[4:12]
    out_ref, row_data, col_data, out_data, row_sem, col_sem, out_sem = refs[12:]
    width = col_data.shape[-1]
    rows, col_count = out_data.shape
    z_place, y_place, x_place, core = (at_ref[i] for i in range(4))

    def order(offset):
        odd = lax.bitwise_and(offset, 1)
        half = lax.shift_right_logical(offset, 1)
        return jnp.where(odd == 1, 2 - half, offset + half)

    row_copies = []
    for core_from, pair in ((core, row_refs[:2]), (1 - core, row_refs[2:])):
        for index, offset in enumerate((0, -1, 1, 2)):
            for turn in range(2):
                zg = lax.bitwise_and(x_place + offset - y_place - z_place, 3)
                yg = 2 * lax.bitwise_xor(lax.bitwise_and(y_place, 1), turn) + core_from
                z_at = order(lax.bitwise_and(zg - z_place, 3))
                y_at = order(lax.bitwise_and(yg - y_place, 3))
                place = jnp.where(core == 0, 4 * y_at + z_at, 4 * z_at + y_at)
                row_copies.append(
                    pltpu.make_async_copy(
                        pair[index // 2].at[index % 2, turn],
                        row_data.at[:, pl.ds(pl.multiple_of(place * width, width), width)],
                        row_sem.at[len(row_copies)],
                    )
                )
    col_copies = []
    for first in range(0, col_count, COL_LOAD):
        part = pl.ds(first, COL_LOAD)
        col_copies.append(
            [
                pltpu.make_async_copy(
                    col_ref.at[:, part],
                    col_data.at[pl.ds(2 * index, 2), part],
                    col_sem.at[len(col_copies), index],
                )
                for index, col_ref in enumerate(col_refs)
            ]
        )
    for copy in row_copies + sum(col_copies, []):
        copy.start()
    for copy in row_copies:
        copy.wait()

    out_copies = []
    out_rows = rows // OUT_PARTS
    for first in range(0, col_count, COL_STEP):
        if first % COL_LOAD == 0:
            for copy in col_copies[first // COL_LOAD]:
                copy.wait()
        part = pl.ds(first, COL_STEP)
        columns = jnp.concatenate([col_data[group, part] for group in range(col_data.shape[0])], axis=1)
        out_data[:, part] = (
            lax.dot_general(
                row_data[...], columns, (((1,), (1,)), ((), ())), preferred_element_type=jnp.float32
            )
            * factor
        )
        for index in range(OUT_PARTS):
            block = pl.ds(index * out_rows, out_rows)
            copy = pltpu.make_async_copy(
                out_data.at[block, part], out_ref.at[block, part], out_sem.at[len(out_copies)]
            )
            copy.start()
            out_copies.append(copy)
    for copy in out_copies:
        copy.wait()


def exchange_block(at, row_parts, pieces):
    offsets, turns, rows, width = row_parts[0].shape
    col_count = pieces[0].shape[1]
    groups = 2 * len(pieces)
    depth = groups * width
    return pl.pallas_call(
        lambda *refs: exchange_kernel(*refs, factor=1.0 / depth),
        in_specs=[pl.BlockSpec(memory_space=pltpu.SMEM)]
        + [pl.BlockSpec(memory_space=pl.ANY)] * (len(row_parts) + len(pieces)),
        out_specs=pl.BlockSpec(memory_space=pl.ANY),
        out_shape=jax.ShapeDtypeStruct((rows, col_count), jnp.float32),
        scratch_shapes=[
            pltpu.VMEM((rows, depth), jnp.bfloat16),
            pltpu.VMEM((groups, col_count, width), jnp.bfloat16),
            pltpu.VMEM((rows, col_count), jnp.float32),
            pltpu.SemaphoreType.DMA((groups,)),
            pltpu.SemaphoreType.DMA((col_count // COL_LOAD, len(pieces))),
            pltpu.SemaphoreType.DMA((col_count // COL_STEP * OUT_PARTS,)),
        ],
        compiler_params=pltpu.CompilerParams(vmem_limit_bytes=EXCHANGE_LIMIT),
        name="exchange",
    )(at, *row_parts, *pieces)


def shards(tiles, tile_owner, pair_rows, pair_cols, orbitals, support):
    tiles_here, _, tile_rows, _ = tiles.shape
    aux_count = lax.axis_size(AUX_AXES)
    bas_count = lax.axis_size(BAS_AXES)
    x_count = lax.axis_size("x")
    block = lax.axis_index(AUX_AXES)
    at = [lax.axis_index(axis) for axis in ALL_AXES]
    x_place, core = at[2:]
    myself = block * bas_count + lax.axis_index(BAS_AXES)
    slots_per_source = 2 * bas_count
    rows_per_part = NBAS // tile_rows // bas_count

    owner_flat = tile_owner[:, 0]
    by_device = (aux_count * bas_count, tiles_here)
    outgoing = half_slots(
        myself[None].astype(jnp.int32),
        tiles,
        owner_flat.reshape(by_device),
        pair_cols.reshape(by_device),
        orbitals,
        support,
        aux_count,
        slots_per_source,
    )
    own = lax.all_to_all(outgoing, AUX_AXES, split_axis=0, concat_axis=0, tiled=True)

    def sources(flat):
        near = lax.dynamic_index_in_dim(flat.reshape(aux_count, x_count, 2, tiles_here), x_place, 1, keepdims=False)
        return jnp.where(core == 0, near, near[:, ::-1]).transpose(1, 0, 2)

    counts, entries = slot_entries(
        sources(owner_flat), sources(pair_rows), block, x_place, core, slots_per_source, rows_per_part
    )
    other = lax.ppermute(own, "core", SWAP)
    local = reduce_over_x(*sum_slots(counts, entries, own, other, rows_per_part))
    pieces, row_parts = gather_both(local)
    return exchange_block(jnp.stack(at).astype(jnp.int32), row_parts, pieces)


def solution(mesh):
    fine = Mesh(mesh.devices.reshape(4, 4, 4, 2), ALL_AXES)
    in_specs = (P(ALL_AXES, None, None, None), P(), P(), P(), P(), P())
    out_specs = P(AUX_AXES, BAS_AXES)
    return jax.shard_map(shards, mesh=fine, in_specs=in_specs, out_specs=out_specs, check_vma=False)
```

```python
import jax
import jax.numpy as jnp
from jax import lax
from jax.experimental import pallas as pl
from jax.experimental.pallas import tpu as pltpu
from jax.sharding import Mesh, PartitionSpec as P

NBAS = 20480
AUX_AXES = ("z", "y")
BAS_AXES = ("x", "core")
ALL_AXES = AUX_AXES + BAS_AXES
TILE_STEP = 32
COL_STEP = 256
COL_LOAD = 512
ROW_STEP = 256
SWAP = [(0, 1), (1, 0)]
VMEM_LIMIT = 56 * 1024 * 1024
SUM_LIMIT = 24 * 1024 * 1024
EXCHANGE_LIMIT = 36 * 1024 * 1024


def half_kernel(self_ref, owner_ref, col_ref, tiles_ref, orbital_ref, support_ref, out_ref, count_ref, kept_ref):
    step = pl.program_id(0)
    aux_here, tile_rows, tile_cols = tiles_ref.shape[1:]
    orbital_count = orbital_ref.shape[0]
    width = aux_here * orbital_count
    block_count = count_ref.shape[0]
    per_block = out_ref.shape[0] // block_count

    @pl.when(step == 0)
    def _():
        for block in range(block_count):
            count_ref[block] = 0
        orbital = lax.broadcasted_iota(jnp.int32, (orbital_count, width), 0)
        column = lax.broadcasted_iota(jnp.int32, (orbital_count, width), 1)
        spread = (lax.rem(column, orbital_count) == orbital).astype(jnp.float32)
        kept_ref[...] = lax.dot_general(
            (support_ref[...] == 1).astype(jnp.float32),
            spread,
            (((0,), (0,)), ((), ())),
            preferred_element_type=jnp.float32,
        )

    row = lax.bitwise_and(self_ref[0], 7)
    lane = lax.broadcasted_iota(jnp.int32, (tile_rows, width), 1)
    for index in range(tiles_ref.shape[0]):
        tile = step * tiles_ref.shape[0] + index
        block = lax.shift_right_logical(owner_ref[row, tile], 3)
        rank = count_ref[block]
        count_ref[block] = rank + 1
        col = col_ref[row, tile]
        chosen = orbital_ref[:, pl.ds(pl.multiple_of(col * tile_cols, tile_cols), tile_cols)]
        product = lax.dot_general(
            tiles_ref[index].reshape(aux_here * tile_rows, tile_cols),
            jnp.concatenate([chosen] * aux_here, axis=0),
            (((1,), (1,)), ((), ())),
            preferred_element_type=jnp.float32,
        )
        half = product[:tile_rows]
        for aux in range(1, aux_here):
            part = product[aux * tile_rows : (aux + 1) * tile_rows]
            half = jnp.where(lane >= aux * orbital_count, part, half)
        kept = kept_ref[pl.ds(col, 1), :] > 0.5
        out_ref[block * per_block + rank] = jnp.where(kept, half, 0.0).astype(out_ref.dtype)


def half_slots(myself, tiles, owners, cols, orbitals, support, block_count, per_block):
    count, aux_here, tile_rows, tile_cols = tiles.shape
    width = aux_here * orbitals.shape[0]
    index_spec = pl.BlockSpec((8, count), lambda i, self_ref: (self_ref[0] // 8, 0), memory_space=pltpu.SMEM)
    return pl.pallas_call(
        half_kernel,
        grid_spec=pltpu.PrefetchScalarGridSpec(
            num_scalar_prefetch=1,
            grid=(count // TILE_STEP,),
            in_specs=[
                index_spec,
                index_spec,
                pl.BlockSpec((TILE_STEP, aux_here, tile_rows, tile_cols), lambda i, _: (i, 0, 0, 0)),
                pl.BlockSpec(orbitals.shape, lambda i, _: (0, 0)),
                pl.BlockSpec(support.shape, lambda i, _: (0, 0)),
            ],
            out_specs=pl.BlockSpec((block_count * per_block, tile_rows, width), lambda i, _: (0, 0, 0)),
            scratch_shapes=[
                pltpu.SMEM((block_count,), jnp.int32),
                pltpu.VMEM((support.shape[1], width), jnp.float32),
            ],
        ),
        out_shape=jax.ShapeDtypeStruct((block_count * per_block, tile_rows, width), jnp.bfloat16),
        compiler_params=pltpu.CompilerParams(vmem_limit_bytes=VMEM_LIMIT),
        name="half_transform",
    )(myself, owners, cols, tiles, orbitals, support)


def sum_kernel(count_ref, list_ref, own_ref, other_ref, *refs):
    out_refs, (total_ref, slots, sem) = refs[:-3], refs[-3:]
    copies = [
        pltpu.make_async_copy(slots_ref, slots.at[side], sem.at[side])
        for side, slots_ref in enumerate((own_ref, other_ref))
    ]
    for copy in copies:
        copy.start()
    total_ref[...] = jnp.zeros_like(total_ref)
    for side, copy in enumerate(copies):
        copy.wait()

        def add(index, carry, side=side):
            entry = list_ref[side, index]
            slot = lax.shift_right_logical(entry, 9)
            place = lax.bitwise_and(entry, 511)
            total_ref[place] += slots[side, slot].astype(jnp.float32)
            return carry

        lax.fori_loop(0, count_ref[side], add, 0)
    first = 0
    for out_ref in out_refs:
        blocks = out_ref.shape[0]
        out_ref[...] = total_ref[pl.ds(first, blocks)].astype(out_ref.dtype)
        first += blocks


def sum_slots(counts, entries, own, other, part):
    tile_shape = own.shape[1:]
    sizes = [part] + [part // 2] * 6
    places = 4 * part
    outs = pl.pallas_call(
        sum_kernel,
        in_specs=[
            pl.BlockSpec(memory_space=pltpu.SMEM),
            pl.BlockSpec(memory_space=pltpu.SMEM),
            pl.BlockSpec(memory_space=pl.ANY),
            pl.BlockSpec(memory_space=pl.ANY),
        ],
        out_specs=[pl.BlockSpec(memory_space=pltpu.VMEM)] * len(sizes),
        out_shape=[jax.ShapeDtypeStruct((size,) + tile_shape, jnp.bfloat16) for size in sizes],
        scratch_shapes=[
            pltpu.VMEM((places,) + tile_shape, jnp.float32),
            pltpu.VMEM((2,) + own.shape, jnp.bfloat16),
            pltpu.SemaphoreType.DMA((2,)),
        ],
        compiler_params=pltpu.CompilerParams(vmem_limit_bytes=SUM_LIMIT),
        name="sum_slots",
    )(counts, entries, own, other)
    return outs


def slot_entries(owners, rows, block, x_place, core, slots_per_source, rows_per_part):
    sides, sources, tiles_here = owners.shape
    hit = lax.shift_right_logical(owners, 3) == block
    mine = jnp.logical_and(hit, (rows // rows_per_part) % 2 == core)
    before = jnp.triu(jnp.ones((tiles_here, tiles_here), jnp.bfloat16), 1)
    flags = jnp.stack([hit, mine]).astype(jnp.bfloat16)
    ahead = jnp.einsum("fkst,tu->fksu", flags, before, preferred_element_type=jnp.float32).astype(jnp.int32)
    slot = jnp.arange(sources, dtype=jnp.int32)[None, :, None] * slots_per_source + ahead[0]
    part = (rows // (2 * rows_per_part) - x_place) & 3
    place = part * rows_per_part + rows % rows_per_part
    mine_counts = jnp.sum(mine.astype(jnp.int32), axis=2)
    earlier = jnp.cumsum(mine_counts, axis=1) - mine_counts
    position = jnp.where(mine, ahead[1] + earlier[:, :, None], -1).reshape(sides, 1, sources * tiles_here)
    packed = (slot * 512 + place).reshape(sides, 1, sources * tiles_here)
    wanted = jnp.arange(sources * slots_per_source, dtype=jnp.int32)[None, :, None]
    entries = jnp.sum(jnp.where(position == wanted, packed, 0), axis=2)
    return jnp.sum(mine_counts, axis=1), entries


def shift(value, axis, by):
    return lax.ppermute(value, axis, [(i, (i + by) % 4) for i in range(4)])


def reduce_over_x(own, p1a, p1b, p2a, p2b, p3a, p3b):
    def add(*values):
        total = sum(value.astype(jnp.float32) for value in values).astype(jnp.bfloat16)
        return total.reshape(-1, total.shape[-1])

    far_a, far_b = shift(p2a, "x", 1), shift(p2b, "x", -1)
    low_b, high_a = shift(p1b, "x", 1), shift(p3a, "x", -1)
    low_a = shift(add(p1a, far_a).reshape(p1a.shape), "x", 1)
    high_b = shift(add(p3b, far_b).reshape(p3b.shape), "x", -1)
    low, high = jnp.concatenate([low_a, low_b]), jnp.concatenate([high_a, high_b])
    return add(own, low, high)


def device(z, y, x, core):
    return ((z * 4 + y) * 4 + x) * 2 + core


def shift_turned(value, second, by):
    pairs = []
    for z in range(4):
        for y in range(4):
            for x in range(4):
                for core in range(2):
                    along_z = (core == 0) != second
                    to_z, to_y = ((z + by) % 4, y) if along_z else (z, (y + by) % 4)
                    pairs.append((device(z, y, x, core), device(to_z, to_y, x, core)))
    return lax.ppermute(value, ALL_AXES, pairs)


def spread_pairs(turn):
    along_x, along_zy = [], []
    for zg in range(4):
        for yg in range(4):
            for z in range(4):
                for high in range(2):
                    y = 2 * high + (yg // 2 ^ turn)
                    x = (zg + y + z) % 4
                    along_x.append((device(zg, yg, z, high), device(zg, yg, x, high)))
                    along_zy.append((device(zg, yg, x, high), device(z, y, x, yg % 2)))
    return along_x, along_zy


def gather_both(local):
    stage = lax.optimization_barrier
    middle = local.shape[0] // 2
    turned = lax.axis_index("y") // 2 == 1
    halves = local[:middle], local[middle:]
    pairs = [spread_pairs(turn) for turn in range(2)]

    low, high = shift_turned(local, False, 1), shift_turned(local, False, -1)
    rows = [lax.ppermute(jnp.where(turned, halves[1 - t], halves[t]), ALL_AXES, pairs[t][0]) for t in range(2)]
    low, high, rows = stage((low, high, rows))

    far_a, far_b = shift_turned(high[:middle], False, -1), shift_turned(low[middle:], False, 1)
    rows = [lax.ppermute(rows[t], ALL_AXES, pairs[t][1]) for t in range(2)]
    near = jnp.stack([local, low])
    near_low, near_high = shift_turned(near, True, 1), shift_turned(near, True, -1)
    far = jnp.stack([high, jnp.concatenate([far_a, far_b])])
    rows = jnp.stack(rows)
    far, rows = stage((far, rows))

    rows_low, rows_high = shift(rows, "x", 1), shift(rows, "x", -1)
    far_low, far_high = shift_turned(far, True, 1), shift_turned(far, True, -1)
    rows_far = jnp.stack([shift(rows_high[0], "x", -1), shift(rows_low[1], "x", 1)])
    near_far, far_far = shift_turned(near_high, True, -1), shift_turned(far_low, True, 1)
    rows_near, rows_far = jnp.stack([rows, rows_low]), jnp.stack([rows_high, rows_far])
    rows = [rows_near, rows_far, lax.ppermute(rows_near, "core", SWAP), lax.ppermute(rows_far, "core", SWAP)]
    return [near, far, near_low, far_low, near_high, far_high, near_far, far_far], rows


def exchange_kernel(at_ref, *refs, factor):
    row_refs, col_refs = refs[:4], refs[4:12]
    out_ref, row_data, col_data, columns, out_data, row_sem, col_sem, out_sem = refs[12:]
    width = col_data.shape[-1]
    rows, col_count = out_data.shape
    z_place, y_place, x_place, core = (at_ref[i] for i in range(4))

    def order(offset):
        odd = lax.bitwise_and(offset, 1)
        half = lax.shift_right_logical(offset, 1)
        return jnp.where(odd == 1, 2 - half, offset + half)

    row_copies = []
    for core_from, pair in ((core, row_refs[:2]), (1 - core, row_refs[2:])):
        for index, offset in enumerate((0, -1, 1, 2)):
            for turn in range(2):
                zg = lax.bitwise_and(x_place + offset - y_place - z_place, 3)
                yg = 2 * lax.bitwise_xor(lax.bitwise_and(y_place, 1), turn) + core_from
                z_at = order(lax.bitwise_and(zg - z_place, 3))
                y_at = order(lax.bitwise_and(yg - y_place, 3))
                place = jnp.where(core == 0, 4 * y_at + z_at, 4 * z_at + y_at)
                row_copies.append(
                    pltpu.make_async_copy(
                        pair[index // 2].at[index % 2, turn],
                        row_data.at[:, pl.ds(pl.multiple_of(place * width, width), width)],
                        row_sem.at[len(row_copies)],
                    )
                )
    col_copies = []
    for first in range(0, col_count, COL_LOAD):
        part = pl.ds(first, COL_LOAD)
        col_copies.append(
            [
                pltpu.make_async_copy(
                    col_ref.at[:, part],
                    col_data.at[pl.ds(2 * index, 2), part],
                    col_sem.at[len(col_copies), index],
                )
                for index, col_ref in enumerate(col_refs)
            ]
        )
    for copy in row_copies + sum(col_copies, []):
        copy.start()
    for copy in row_copies:
        copy.wait()

    row_blocks = rows // ROW_STEP

    def out_copy(first, block, index):
        place = pl.ds(pl.multiple_of(block * ROW_STEP, ROW_STEP), ROW_STEP), pl.ds(first, COL_STEP)
        return pltpu.make_async_copy(out_data.at[place], out_ref.at[place], out_sem.at[index, block])

    for index, first in enumerate(range(0, col_count, COL_STEP)):
        if first % COL_LOAD == 0:
            for copy in col_copies[first // COL_LOAD]:
                copy.wait()
        part = pl.ds(first, COL_STEP)
        for group in range(col_data.shape[0]):
            columns[:, pl.ds(group * width, width)] = col_data[group, part]

        def multiply(block, carry, index=index, first=first, part=part):
            place = pl.ds(pl.multiple_of(block * ROW_STEP, ROW_STEP), ROW_STEP)
            out_data[place, part] = (
                lax.dot_general(
                    row_data[place], columns[...], (((1,), (1,)), ((), ())), preferred_element_type=jnp.float32
                )
                * factor
            )
            out_copy(first, block, index).start()
            return carry

        lax.fori_loop(0, row_blocks, multiply, 0)

    for index, first in enumerate(range(0, col_count, COL_STEP)):
        for block in range(row_blocks):
            out_copy(first, block, index).wait()


def exchange_block(at, row_parts, pieces):
    offsets, turns, rows, width = row_parts[0].shape
    col_count = pieces[0].shape[1]
    groups = 2 * len(pieces)
    depth = groups * width
    return pl.pallas_call(
        lambda *refs: exchange_kernel(*refs, factor=1.0 / depth),
        in_specs=[pl.BlockSpec(memory_space=pltpu.SMEM)]
        + [pl.BlockSpec(memory_space=pl.ANY)] * (len(row_parts) + len(pieces)),
        out_specs=pl.BlockSpec(memory_space=pl.ANY),
        out_shape=jax.ShapeDtypeStruct((rows, col_count), jnp.float32),
        scratch_shapes=[
            pltpu.VMEM((rows, depth), jnp.bfloat16),
            pltpu.VMEM((groups, col_count, width), jnp.bfloat16),
            pltpu.VMEM((COL_STEP, depth), jnp.bfloat16),
            pltpu.VMEM((rows, col_count), jnp.float32),
            pltpu.SemaphoreType.DMA((groups,)),
            pltpu.SemaphoreType.DMA((col_count // COL_LOAD, len(pieces))),
            pltpu.SemaphoreType.DMA((col_count // COL_STEP, rows // ROW_STEP)),
        ],
        compiler_params=pltpu.CompilerParams(vmem_limit_bytes=EXCHANGE_LIMIT),
        name="exchange",
    )(at, *row_parts, *pieces)


def shards(tiles, tile_owner, pair_rows, pair_cols, orbitals, support):
    tiles_here, _, tile_rows, _ = tiles.shape
    aux_count = lax.axis_size(AUX_AXES)
    bas_count = lax.axis_size(BAS_AXES)
    x_count = lax.axis_size("x")
    block = lax.axis_index(AUX_AXES)
    at = [lax.axis_index(axis) for axis in ALL_AXES]
    x_place, core = at[2:]
    myself = block * bas_count + lax.axis_index(BAS_AXES)
    slots_per_source = 2 * bas_count
    rows_per_part = NBAS // tile_rows // bas_count

    owner_flat = tile_owner[:, 0]
    by_device = (aux_count * bas_count, tiles_here)
    outgoing = half_slots(
        myself[None].astype(jnp.int32),
        tiles,
        owner_flat.reshape(by_device),
        pair_cols.reshape(by_device),
        orbitals,
        support,
        aux_count,
        slots_per_source,
    )
    own = lax.all_to_all(outgoing, AUX_AXES, split_axis=0, concat_axis=0, tiled=True)

    def sources(flat):
        near = lax.dynamic_index_in_dim(flat.reshape(aux_count, x_count, 2, tiles_here), x_place, 1, keepdims=False)
        return jnp.where(core == 0, near, near[:, ::-1]).transpose(1, 0, 2)

    counts, entries = slot_entries(
        sources(owner_flat), sources(pair_rows), block, x_place, core, slots_per_source, rows_per_part
    )
    other = lax.ppermute(own, "core", SWAP)
    local = reduce_over_x(*sum_slots(counts, entries, own, other, rows_per_part))
    pieces, row_parts = gather_both(local)
    return exchange_block(jnp.stack(at).astype(jnp.int32), row_parts, pieces)


def solution(mesh):
    fine = Mesh(mesh.devices.reshape(4, 4, 4, 2), ALL_AXES)
    in_specs = (P(ALL_AXES, None, None, None), P(), P(), P(), P(), P())
    out_specs = P(AUX_AXES, BAS_AXES)
    return jax.shard_map(shards, mesh=fine, in_specs=in_specs, out_specs=out_specs, check_vma=False)
```

```python
import jax
import jax.numpy as jnp
from jax import lax
from jax.experimental import pallas as pl
from jax.experimental.pallas import tpu as pltpu
from jax.sharding import Mesh, PartitionSpec as P

NBAS = 20480
AUX_AXES = ("z", "y")
BAS_AXES = ("x", "core")
ALL_AXES = AUX_AXES + BAS_AXES
TILE_STEP = 32
COL_STEP = 256
COL_LOAD = 512
OUT_PARTS = 4
SWAP = [(0, 1), (1, 0)]
VMEM_LIMIT = 56 * 1024 * 1024
SUM_LIMIT = 24 * 1024 * 1024
EXCHANGE_LIMIT = 36 * 1024 * 1024


def half_kernel(self_ref, owner_ref, col_ref, tiles_ref, orbital_ref, support_ref, out_ref, count_ref, kept_ref):
    step = pl.program_id(0)
    aux_here, tile_rows, tile_cols = tiles_ref.shape[1:]
    orbital_count = orbital_ref.shape[0]
    width = aux_here * orbital_count
    block_count = count_ref.shape[0]
    per_block = out_ref.shape[0] // block_count

    @pl.when(step == 0)
    def _():
        for block in range(block_count):
            count_ref[block] = 0
        orbital = lax.broadcasted_iota(jnp.int32, (orbital_count, width), 0)
        column = lax.broadcasted_iota(jnp.int32, (orbital_count, width), 1)
        spread = (lax.rem(column, orbital_count) == orbital).astype(jnp.float32)
        kept_ref[...] = lax.dot_general(
            (support_ref[...] == 1).astype(jnp.float32),
            spread,
            (((0,), (0,)), ((), ())),
            preferred_element_type=jnp.float32,
        )

    row = lax.bitwise_and(self_ref[0], 7)
    lane = lax.broadcasted_iota(jnp.int32, (tile_rows, width), 1)
    for index in range(tiles_ref.shape[0]):
        tile = step * tiles_ref.shape[0] + index
        block = lax.shift_right_logical(owner_ref[row, tile], 3)
        rank = count_ref[block]
        count_ref[block] = rank + 1
        col = col_ref[row, tile]
        chosen = orbital_ref[:, pl.ds(pl.multiple_of(col * tile_cols, tile_cols), tile_cols)]
        product = lax.dot_general(
            tiles_ref[index].reshape(aux_here * tile_rows, tile_cols),
            jnp.concatenate([chosen] * aux_here, axis=0),
            (((1,), (1,)), ((), ())),
            preferred_element_type=jnp.float32,
        )
        half = product[:tile_rows]
        for aux in range(1, aux_here):
            part = product[aux * tile_rows : (aux + 1) * tile_rows]
            half = jnp.where(lane >= aux * orbital_count, part, half)
        kept = kept_ref[pl.ds(col, 1), :] > 0.5
        out_ref[block * per_block + rank] = jnp.where(kept, half, 0.0).astype(out_ref.dtype)


def half_slots(myself, tiles, owners, cols, orbitals, support, block_count, per_block):
    count, aux_here, tile_rows, tile_cols = tiles.shape
    width = aux_here * orbitals.shape[0]
    index_spec = pl.BlockSpec((8, count), lambda i, self_ref: (self_ref[0] // 8, 0), memory_space=pltpu.SMEM)
    return pl.pallas_call(
        half_kernel,
        grid_spec=pltpu.PrefetchScalarGridSpec(
            num_scalar_prefetch=1,
            grid=(count // TILE_STEP,),
            in_specs=[
                index_spec,
                index_spec,
                pl.BlockSpec((TILE_STEP, aux_here, tile_rows, tile_cols), lambda i, _: (i, 0, 0, 0)),
                pl.BlockSpec(orbitals.shape, lambda i, _: (0, 0)),
                pl.BlockSpec(support.shape, lambda i, _: (0, 0)),
            ],
            out_specs=pl.BlockSpec((block_count * per_block, tile_rows, width), lambda i, _: (0, 0, 0)),
            scratch_shapes=[
                pltpu.SMEM((block_count,), jnp.int32),
                pltpu.VMEM((support.shape[1], width), jnp.float32),
            ],
        ),
        out_shape=jax.ShapeDtypeStruct((block_count * per_block, tile_rows, width), jnp.bfloat16),
        compiler_params=pltpu.CompilerParams(vmem_limit_bytes=VMEM_LIMIT),
        name="half_transform",
    )(myself, owners, cols, tiles, orbitals, support)


def sum_kernel(count_ref, list_ref, own_ref, other_ref, *refs):
    out_refs, (total_ref, slots, sem) = refs[:-3], refs[-3:]
    copies = [
        pltpu.make_async_copy(slots_ref, slots.at[side], sem.at[side])
        for side, slots_ref in enumerate((own_ref, other_ref))
    ]
    for copy in copies:
        copy.start()
    total_ref[...] = jnp.zeros_like(total_ref)
    for side, copy in enumerate(copies):
        copy.wait()

        def add(index, carry, side=side):
            entry = list_ref[side, index]
            slot = lax.shift_right_logical(entry, 9)
            place = lax.bitwise_and(entry, 511)
            total_ref[place] += slots[side, slot].astype(jnp.float32)
            return carry

        lax.fori_loop(0, count_ref[side], add, 0)
    first = 0
    for out_ref in out_refs:
        blocks = out_ref.shape[0]
        out_ref[...] = total_ref[pl.ds(first, blocks)].astype(out_ref.dtype)
        first += blocks


def sum_slots(counts, entries, own, other, part):
    tile_shape = own.shape[1:]
    sizes = [part] + [part // 2] * 6
    places = 4 * part
    outs = pl.pallas_call(
        sum_kernel,
        in_specs=[
            pl.BlockSpec(memory_space=pltpu.SMEM),
            pl.BlockSpec(memory_space=pltpu.SMEM),
            pl.BlockSpec(memory_space=pl.ANY),
            pl.BlockSpec(memory_space=pl.ANY),
        ],
        out_specs=[pl.BlockSpec(memory_space=pltpu.VMEM)] * len(sizes),
        out_shape=[jax.ShapeDtypeStruct((size,) + tile_shape, jnp.bfloat16) for size in sizes],
        scratch_shapes=[
            pltpu.VMEM((places,) + tile_shape, jnp.float32),
            pltpu.VMEM((2,) + own.shape, jnp.bfloat16),
            pltpu.SemaphoreType.DMA((2,)),
        ],
        compiler_params=pltpu.CompilerParams(vmem_limit_bytes=SUM_LIMIT),
        name="sum_slots",
    )(counts, entries, own, other)
    return outs


def slot_entries(owners, rows, block, x_place, core, slots_per_source, rows_per_part):
    sides, sources, tiles_here = owners.shape
    hit = lax.shift_right_logical(owners, 3) == block
    mine = jnp.logical_and(hit, (rows // rows_per_part) % 2 == core)
    before = jnp.triu(jnp.ones((tiles_here, tiles_here), jnp.bfloat16), 1)
    flags = jnp.stack([hit, mine]).astype(jnp.bfloat16)
    ahead = jnp.einsum("fkst,tu->fksu", flags, before, preferred_element_type=jnp.float32).astype(jnp.int32)
    slot = jnp.arange(sources, dtype=jnp.int32)[None, :, None] * slots_per_source + ahead[0]
    part = (rows // (2 * rows_per_part) - x_place) & 3
    place = part * rows_per_part + rows % rows_per_part
    mine_counts = jnp.sum(mine.astype(jnp.int32), axis=2)
    earlier = jnp.cumsum(mine_counts, axis=1) - mine_counts
    position = jnp.where(mine, ahead[1] + earlier[:, :, None], -1).reshape(sides, 1, sources * tiles_here)
    packed = (slot * 512 + place).reshape(sides, 1, sources * tiles_here)
    wanted = jnp.arange(sources * slots_per_source, dtype=jnp.int32)[None, :, None]
    entries = jnp.sum(jnp.where(position == wanted, packed, 0), axis=2)
    return jnp.sum(mine_counts, axis=1), entries


def shift(value, axis, by):
    return lax.ppermute(value, axis, [(i, (i + by) % 4) for i in range(4)])


def reduce_over_x(own, p1a, p1b, p2a, p2b, p3a, p3b):
    def add(*values):
        total = sum(value.astype(jnp.float32) for value in values).astype(jnp.bfloat16)
        return total.reshape(-1, total.shape[-1])

    far_a, far_b = shift(p2a, "x", 1), shift(p2b, "x", -1)
    low_b, high_a = shift(p1b, "x", 1), shift(p3a, "x", -1)
    low_a = shift(add(p1a, far_a).reshape(p1a.shape), "x", 1)
    high_b = shift(add(p3b, far_b).reshape(p3b.shape), "x", -1)
    low, high = jnp.concatenate([low_a, low_b]), jnp.concatenate([high_a, high_b])
    return add(own, low, high)


def device(z, y, x, core):
    return ((z * 4 + y) * 4 + x) * 2 + core


def shift_turned(value, second, by):
    pairs = []
    for z in range(4):
        for y in range(4):
            for x in range(4):
                for core in range(2):
                    along_z = (core == 0) != second
                    to_z, to_y = ((z + by) % 4, y) if along_z else (z, (y + by) % 4)
                    pairs.append((device(z, y, x, core), device(to_z, to_y, x, core)))
    return lax.ppermute(value, ALL_AXES, pairs)


def spread_pairs(turn):
    along_x, along_zy = [], []
    for zg in range(4):
        for yg in range(4):
            for z in range(4):
                for high in range(2):
                    y = 2 * high + (yg // 2 ^ turn)
                    x = (zg + y + z) % 4
                    along_x.append((device(zg, yg, z, high), device(zg, yg, x, high)))
                    along_zy.append((device(zg, yg, x, high), device(z, y, x, yg % 2)))
    return along_x, along_zy


def gather_both(local):
    stage = lax.optimization_barrier
    middle = local.shape[0] // 2
    turned = lax.axis_index("y") // 2 == 1
    halves = local[:middle], local[middle:]
    pairs = [spread_pairs(turn) for turn in range(2)]

    low, high = shift_turned(local, False, 1), shift_turned(local, False, -1)
    rows = [lax.ppermute(jnp.where(turned, halves[1 - t], halves[t]), ALL_AXES, pairs[t][0]) for t in range(2)]
    low, high, rows = stage((low, high, rows))

    far_a, far_b = shift_turned(high[:middle], False, -1), shift_turned(low[middle:], False, 1)
    near = jnp.stack([local, low])
    near_low, near_high = shift_turned(near, True, 1), shift_turned(near, True, -1)
    far_a, far_b, rows = stage((far_a, far_b, rows))
    rows = jnp.stack([lax.ppermute(rows[t], ALL_AXES, pairs[t][1]) for t in range(2)])
    far = jnp.stack([high, jnp.concatenate([far_a, far_b])])

    rows_low, rows_high = shift(rows, "x", 1), shift(rows, "x", -1)
    far_low, far_high = shift_turned(far, True, 1), shift_turned(far, True, -1)
    rows_far = jnp.stack([shift(rows_high[0], "x", -1), shift(rows_low[1], "x", 1)])
    near_far, far_far = shift_turned(near_high, True, -1), shift_turned(far_low, True, 1)
    rows_near, rows_far = jnp.stack([rows, rows_low]), jnp.stack([rows_high, rows_far])
    rows = [rows_near, rows_far, lax.ppermute(rows_near, "core", SWAP), lax.ppermute(rows_far, "core", SWAP)]
    return [near, far, near_low, far_low, near_high, far_high, near_far, far_far], rows


def exchange_kernel(at_ref, *refs, factor):
    row_refs, col_refs = refs[:4], refs[4:12]
    out_ref, row_data, col_data, out_data, row_sem, col_sem, out_sem = refs[12:]
    width = col_data.shape[-1]
    rows, col_count = out_data.shape
    z_place, y_place, x_place, core = (at_ref[i] for i in range(4))

    def order(offset):
        odd = lax.bitwise_and(offset, 1)
        half = lax.shift_right_logical(offset, 1)
        return jnp.where(odd == 1, 2 - half, offset + half)

    row_copies = []
    for core_from, pair in ((core, row_refs[:2]), (1 - core, row_refs[2:])):
        for index, offset in enumerate((0, -1, 1, 2)):
            for turn in range(2):
                zg = lax.bitwise_and(x_place + offset - y_place - z_place, 3)
                yg = 2 * lax.bitwise_xor(lax.bitwise_and(y_place, 1), turn) + core_from
                z_at = order(lax.bitwise_and(zg - z_place, 3))
                y_at = order(lax.bitwise_and(yg - y_place, 3))
                place = jnp.where(core == 0, 4 * y_at + z_at, 4 * z_at + y_at)
                row_copies.append(
                    pltpu.make_async_copy(
                        pair[index // 2].at[index % 2, turn],
                        row_data.at[:, pl.ds(pl.multiple_of(place * width, width), width)],
                        row_sem.at[len(row_copies)],
                    )
                )
    col_copies = []
    for first in range(0, col_count, COL_LOAD):
        part = pl.ds(first, COL_LOAD)
        col_copies.append(
            [
                pltpu.make_async_copy(
                    col_ref.at[:, part],
                    col_data.at[pl.ds(2 * index, 2), part],
                    col_sem.at[len(col_copies), index],
                )
                for index, col_ref in enumerate(col_refs)
            ]
        )
    for copy in row_copies + sum(col_copies, []):
        copy.start()
    for copy in row_copies:
        copy.wait()

    out_copies = []
    out_rows = rows // OUT_PARTS
    for first in range(0, col_count, COL_STEP):
        if first % COL_LOAD == 0:
            for copy in col_copies[first // COL_LOAD]:
                copy.wait()
        part = pl.ds(first, COL_STEP)
        columns = jnp.concatenate([col_data[group, part] for group in range(col_data.shape[0])], axis=1)
        out_data[:, part] = (
            lax.dot_general(
                row_data[...], columns, (((1,), (1,)), ((), ())), preferred_element_type=jnp.float32
            )
            * factor
        )
        for index in range(OUT_PARTS):
            block = pl.ds(index * out_rows, out_rows)
            copy = pltpu.make_async_copy(
                out_data.at[block, part], out_ref.at[block, part], out_sem.at[len(out_copies)]
            )
            copy.start()
            out_copies.append(copy)
    for copy in out_copies:
        copy.wait()


def exchange_block(at, row_parts, pieces):
    offsets, turns, rows, width = row_parts[0].shape
    col_count = pieces[0].shape[1]
    groups = 2 * len(pieces)
    depth = groups * width
    return pl.pallas_call(
        lambda *refs: exchange_kernel(*refs, factor=1.0 / depth),
        in_specs=[pl.BlockSpec(memory_space=pltpu.SMEM)]
        + [pl.BlockSpec(memory_space=pl.ANY)] * (len(row_parts) + len(pieces)),
        out_specs=pl.BlockSpec(memory_space=pl.ANY),
        out_shape=jax.ShapeDtypeStruct((rows, col_count), jnp.float32),
        scratch_shapes=[
            pltpu.VMEM((rows, depth), jnp.bfloat16),
            pltpu.VMEM((groups, col_count, width), jnp.bfloat16),
            pltpu.VMEM((rows, col_count), jnp.float32),
            pltpu.SemaphoreType.DMA((groups,)),
            pltpu.SemaphoreType.DMA((col_count // COL_LOAD, len(pieces))),
            pltpu.SemaphoreType.DMA((col_count // COL_STEP * OUT_PARTS,)),
        ],
        compiler_params=pltpu.CompilerParams(vmem_limit_bytes=EXCHANGE_LIMIT),
        name="exchange",
    )(at, *row_parts, *pieces)


def shards(tiles, tile_owner, pair_rows, pair_cols, orbitals, support):
    tiles_here, _, tile_rows, _ = tiles.shape
    aux_count = lax.axis_size(AUX_AXES)
    bas_count = lax.axis_size(BAS_AXES)
    x_count = lax.axis_size("x")
    block = lax.axis_index(AUX_AXES)
    at = [lax.axis_index(axis) for axis in ALL_AXES]
    x_place, core = at[2:]
    myself = block * bas_count + lax.axis_index(BAS_AXES)
    slots_per_source = 2 * bas_count
    rows_per_part = NBAS // tile_rows // bas_count

    owner_flat = tile_owner[:, 0]
    by_device = (aux_count * bas_count, tiles_here)
    outgoing = half_slots(
        myself[None].astype(jnp.int32),
        tiles,
        owner_flat.reshape(by_device),
        pair_cols.reshape(by_device),
        orbitals,
        support,
        aux_count,
        slots_per_source,
    )
    own = lax.all_to_all(outgoing, AUX_AXES, split_axis=0, concat_axis=0, tiled=True)

    def sources(flat):
        near = lax.dynamic_index_in_dim(flat.reshape(aux_count, x_count, 2, tiles_here), x_place, 1, keepdims=False)
        return jnp.where(core == 0, near, near[:, ::-1]).transpose(1, 0, 2)

    counts, entries = slot_entries(
        sources(owner_flat), sources(pair_rows), block, x_place, core, slots_per_source, rows_per_part
    )
    other = lax.ppermute(own, "core", SWAP)
    local = reduce_over_x(*sum_slots(counts, entries, own, other, rows_per_part))
    pieces, row_parts = gather_both(local)
    return exchange_block(jnp.stack(at).astype(jnp.int32), row_parts, pieces)


def solution(mesh):
    fine = Mesh(mesh.devices.reshape(4, 4, 4, 2), ALL_AXES)
    in_specs = (P(ALL_AXES, None, None, None), P(), P(), P(), P(), P())
    out_specs = P(AUX_AXES, BAS_AXES)
    return jax.shard_map(shards, mesh=fine, in_specs=in_specs, out_specs=out_specs, check_vma=False)
```

```python
import jax
import jax.numpy as jnp
from jax import lax
from jax.experimental import pallas as pl
from jax.experimental.pallas import tpu as pltpu
from jax.sharding import Mesh, PartitionSpec as P

NBAS = 20480
AUX_AXES = ("z", "y")
BAS_AXES = ("x", "core")
ALL_AXES = AUX_AXES + BAS_AXES
TILE_STEP = 32
COL_STEP = 256
COL_LOAD = 512
OUT_PARTS = 4
SWAP = [(0, 1), (1, 0)]
VMEM_LIMIT = 56 * 1024 * 1024
SUM_LIMIT = 24 * 1024 * 1024
EXCHANGE_LIMIT = 36 * 1024 * 1024


def half_kernel(self_ref, owner_ref, col_ref, tiles_ref, orbital_ref, support_ref, out_ref, count_ref, kept_ref):
    step = pl.program_id(0)
    aux_here, tile_rows, tile_cols = tiles_ref.shape[1:]
    orbital_count = orbital_ref.shape[0]
    width = aux_here * orbital_count
    block_count = count_ref.shape[0]
    per_block = out_ref.shape[0] // block_count

    @pl.when(step == 0)
    def _():
        for block in range(block_count):
            count_ref[block] = 0
        orbital = lax.broadcasted_iota(jnp.int32, (orbital_count, width), 0)
        column = lax.broadcasted_iota(jnp.int32, (orbital_count, width), 1)
        spread = (lax.rem(column, orbital_count) == orbital).astype(jnp.float32)
        kept_ref[...] = lax.dot_general(
            (support_ref[...] == 1).astype(jnp.float32),
            spread,
            (((0,), (0,)), ((), ())),
            preferred_element_type=jnp.float32,
        )

    row = lax.bitwise_and(self_ref[0], 7)
    lane = lax.broadcasted_iota(jnp.int32, (tile_rows, width), 1)
    for index in range(tiles_ref.shape[0]):
        tile = step * tiles_ref.shape[0] + index
        block = lax.shift_right_logical(owner_ref[row, tile], 3)
        rank = count_ref[block]
        count_ref[block] = rank + 1
        col = col_ref[row, tile]
        chosen = orbital_ref[:, pl.ds(pl.multiple_of(col * tile_cols, tile_cols), tile_cols)]
        product = lax.dot_general(
            tiles_ref[index].reshape(aux_here * tile_rows, tile_cols),
            jnp.concatenate([chosen] * aux_here, axis=0),
            (((1,), (1,)), ((), ())),
            preferred_element_type=jnp.float32,
        )
        half = product[:tile_rows]
        for aux in range(1, aux_here):
            part = product[aux * tile_rows : (aux + 1) * tile_rows]
            half = jnp.where(lane >= aux * orbital_count, part, half)
        kept = kept_ref[pl.ds(col, 1), :] > 0.5
        out_ref[block * per_block + rank] = jnp.where(kept, half, 0.0).astype(out_ref.dtype)


def half_slots(myself, tiles, owners, cols, orbitals, support, block_count, per_block):
    count, aux_here, tile_rows, tile_cols = tiles.shape
    width = aux_here * orbitals.shape[0]
    index_spec = pl.BlockSpec((8, count), lambda i, self_ref: (self_ref[0] // 8, 0), memory_space=pltpu.SMEM)
    return pl.pallas_call(
        half_kernel,
        grid_spec=pltpu.PrefetchScalarGridSpec(
            num_scalar_prefetch=1,
            grid=(count // TILE_STEP,),
            in_specs=[
                index_spec,
                index_spec,
                pl.BlockSpec((TILE_STEP, aux_here, tile_rows, tile_cols), lambda i, _: (i, 0, 0, 0)),
                pl.BlockSpec(orbitals.shape, lambda i, _: (0, 0)),
                pl.BlockSpec(support.shape, lambda i, _: (0, 0)),
            ],
            out_specs=pl.BlockSpec((block_count * per_block, tile_rows, width), lambda i, _: (0, 0, 0)),
            scratch_shapes=[
                pltpu.SMEM((block_count,), jnp.int32),
                pltpu.VMEM((support.shape[1], width), jnp.float32),
            ],
        ),
        out_shape=jax.ShapeDtypeStruct((block_count * per_block, tile_rows, width), jnp.bfloat16),
        compiler_params=pltpu.CompilerParams(vmem_limit_bytes=VMEM_LIMIT),
        name="half_transform",
    )(myself, owners, cols, tiles, orbitals, support)


def sum_kernel(count_ref, list_ref, own_ref, other_ref, *refs):
    out_refs, (total_ref, slots, sem) = refs[:-3], refs[-3:]
    copies = [
        pltpu.make_async_copy(slots_ref, slots.at[side], sem.at[side])
        for side, slots_ref in enumerate((own_ref, other_ref))
    ]
    for copy in copies:
        copy.start()
    total_ref[...] = jnp.zeros_like(total_ref)
    for side, copy in enumerate(copies):
        copy.wait()

        def add(index, carry, side=side):
            entry = list_ref[side, index]
            slot = lax.shift_right_logical(entry, 9)
            place = lax.bitwise_and(entry, 511)
            total_ref[place] += slots[side, slot].astype(jnp.float32)
            return carry

        lax.fori_loop(0, count_ref[side], add, 0)
    first = 0
    for out_ref in out_refs:
        blocks = out_ref.shape[0]
        out_ref[...] = total_ref[pl.ds(first, blocks)].astype(out_ref.dtype)
        first += blocks


def sum_slots(counts, entries, own, other, part):
    tile_shape = own.shape[1:]
    sizes = [part] + [part // 2] * 6
    places = 4 * part
    outs = pl.pallas_call(
        sum_kernel,
        in_specs=[
            pl.BlockSpec(memory_space=pltpu.SMEM),
            pl.BlockSpec(memory_space=pltpu.SMEM),
            pl.BlockSpec(memory_space=pl.ANY),
            pl.BlockSpec(memory_space=pl.ANY),
        ],
        out_specs=[pl.BlockSpec(memory_space=pltpu.VMEM)] * len(sizes),
        out_shape=[jax.ShapeDtypeStruct((size,) + tile_shape, jnp.bfloat16) for size in sizes],
        scratch_shapes=[
            pltpu.VMEM((places,) + tile_shape, jnp.float32),
            pltpu.VMEM((2,) + own.shape, jnp.bfloat16),
            pltpu.SemaphoreType.DMA((2,)),
        ],
        compiler_params=pltpu.CompilerParams(vmem_limit_bytes=SUM_LIMIT),
        name="sum_slots",
    )(counts, entries, own, other)
    return outs


def slot_entries(owners, rows, block, x_place, core, slots_per_source, rows_per_part):
    sides, sources, tiles_here = owners.shape
    hit = lax.shift_right_logical(owners, 3) == block
    mine = jnp.logical_and(hit, (rows // rows_per_part) % 2 == core)
    before = jnp.triu(jnp.ones((tiles_here, tiles_here), jnp.bfloat16), 1)
    flags = jnp.stack([hit, mine]).astype(jnp.bfloat16)
    ahead = jnp.einsum("fkst,tu->fksu", flags, before, preferred_element_type=jnp.float32).astype(jnp.int32)
    slot = jnp.arange(sources, dtype=jnp.int32)[None, :, None] * slots_per_source + ahead[0]
    part = (rows // (2 * rows_per_part) - x_place) & 3
    place = part * rows_per_part + rows % rows_per_part
    mine_counts = jnp.sum(mine.astype(jnp.int32), axis=2)
    earlier = jnp.cumsum(mine_counts, axis=1) - mine_counts
    position = jnp.where(mine, ahead[1] + earlier[:, :, None], -1).reshape(sides, 1, sources * tiles_here)
    packed = (slot * 512 + place).reshape(sides, 1, sources * tiles_here)
    wanted = jnp.arange(sources * slots_per_source, dtype=jnp.int32)[None, :, None]
    entries = jnp.sum(jnp.where(position == wanted, packed, 0), axis=2)
    return jnp.sum(mine_counts, axis=1), entries


def shift(value, axis, by):
    return lax.ppermute(value, axis, [(i, (i + by) % 4) for i in range(4)])


def reduce_over_x(own, p1a, p1b, p2a, p2b, p3a, p3b):
    def add(*values):
        total = sum(value.astype(jnp.float32) for value in values).astype(jnp.bfloat16)
        return total.reshape(-1, total.shape[-1])

    far_a, far_b = shift(p2a, "x", 1), shift(p2b, "x", -1)
    low_b, high_a = shift(p1b, "x", 1), shift(p3a, "x", -1)
    low_a = shift(add(p1a, far_a).reshape(p1a.shape), "x", 1)
    high_b = shift(add(p3b, far_b).reshape(p3b.shape), "x", -1)
    low, high = jnp.concatenate([low_a, low_b]), jnp.concatenate([high_a, high_b])
    return add(own, low, high)


def device(z, y, x, core):
    return ((z * 4 + y) * 4 + x) * 2 + core


def shift_turned(value, second, by):
    pairs = []
    for z in range(4):
        for y in range(4):
            for x in range(4):
                for core in range(2):
                    along_z = (core == 0) != second
                    to_z, to_y = ((z + by) % 4, y) if along_z else (z, (y + by) % 4)
                    pairs.append((device(z, y, x, core), device(to_z, to_y, x, core)))
    return lax.ppermute(value, ALL_AXES, pairs)


def spread_pairs(turn):
    along_x, along_zy = [], []
    for zg in range(4):
        for yg in range(4):
            for z in range(4):
                for high in range(2):
                    y = 2 * high + (yg // 2 ^ turn)
                    x = (zg + y + z) % 4
                    along_x.append((device(zg, yg, z, high), device(zg, yg, x, high)))
                    along_zy.append((device(zg, yg, x, high), device(z, y, x, yg % 2)))
    return along_x, along_zy


def gather_both(local):
    stage = lax.optimization_barrier
    middle = local.shape[0] // 2
    turned = lax.axis_index("y") // 2 == 1
    halves = local[:middle], local[middle:]
    pairs = [spread_pairs(turn) for turn in range(2)]

    low, high = shift_turned(local, False, 1), shift_turned(local, False, -1)
    rows = [lax.ppermute(jnp.where(turned, halves[1 - t], halves[t]), ALL_AXES, pairs[t][0]) for t in range(2)]
    low, high, rows = stage((low, high, rows))

    far_a, far_b = shift_turned(high[:middle], False, -1), shift_turned(low[middle:], False, 1)
    near = jnp.stack([local, low])
    near_low, near_high = shift_turned(near, True, 1), shift_turned(near, True, -1)
    rows = jnp.stack([lax.ppermute(rows[t], ALL_AXES, pairs[t][1]) for t in range(2)])
    far = jnp.stack([high, jnp.concatenate([far_a, far_b])])
    near_low, near_high, far, rows = stage((near_low, near_high, far, rows))

    rows_low, rows_high = shift(rows, "x", 1), shift(rows, "x", -1)
    far_low, far_high = shift_turned(far, True, 1), shift_turned(far, True, -1)
    far_low, far_high, rows_low, rows_high = stage((far_low, far_high, rows_low, rows_high))

    near_far, far_far = shift_turned(near_high, True, -1), shift_turned(far_low, True, 1)
    rows_far = jnp.stack([shift(rows_high[0], "x", -1), shift(rows_low[1], "x", 1)])
    rows_near, rows_far = jnp.stack([rows, rows_low]), jnp.stack([rows_high, rows_far])
    rows = [rows_near, rows_far, lax.ppermute(rows_near, "core", SWAP), lax.ppermute(rows_far, "core", SWAP)]
    return [near, far, near_low, far_low, near_high, far_high, near_far, far_far], rows


def exchange_kernel(at_ref, *refs, factor):
    row_refs, col_refs = refs[:4], refs[4:12]
    out_ref, row_data, col_data, out_data, row_sem, col_sem, out_sem = refs[12:]
    width = col_data.shape[-1]
    rows, col_count = out_data.shape
    z_place, y_place, x_place, core = (at_ref[i] for i in range(4))

    def order(offset):
        odd = lax.bitwise_and(offset, 1)
        half = lax.shift_right_logical(offset, 1)
        return jnp.where(odd == 1, 2 - half, offset + half)

    row_copies = []
    for core_from, pair in ((core, row_refs[:2]), (1 - core, row_refs[2:])):
        for index, offset in enumerate((0, -1, 1, 2)):
            for turn in range(2):
                zg = lax.bitwise_and(x_place + offset - y_place - z_place, 3)
                yg = 2 * lax.bitwise_xor(lax.bitwise_and(y_place, 1), turn) + core_from
                z_at = order(lax.bitwise_and(zg - z_place, 3))
                y_at = order(lax.bitwise_and(yg - y_place, 3))
                place = jnp.where(core == 0, 4 * y_at + z_at, 4 * z_at + y_at)
                row_copies.append(
                    pltpu.make_async_copy(
                        pair[index // 2].at[index % 2, turn],
                        row_data.at[:, pl.ds(pl.multiple_of(place * width, width), width)],
                        row_sem.at[len(row_copies)],
                    )
                )
    col_copies = []
    for first in range(0, col_count, COL_LOAD):
        part = pl.ds(first, COL_LOAD)
        col_copies.append(
            [
                pltpu.make_async_copy(
                    col_ref.at[:, part],
                    col_data.at[pl.ds(2 * index, 2), part],
                    col_sem.at[len(col_copies), index],
                )
                for index, col_ref in enumerate(col_refs)
            ]
        )
    for copy in row_copies + sum(col_copies, []):
        copy.start()
    for copy in row_copies:
        copy.wait()

    out_copies = []
    out_rows = rows // OUT_PARTS
    for first in range(0, col_count, COL_STEP):
        if first % COL_LOAD == 0:
            for copy in col_copies[first // COL_LOAD]:
                copy.wait()
        part = pl.ds(first, COL_STEP)
        columns = jnp.concatenate([col_data[group, part] for group in range(col_data.shape[0])], axis=1)
        out_data[:, part] = (
            lax.dot_general(
                row_data[...], columns, (((1,), (1,)), ((), ())), preferred_element_type=jnp.float32
            )
            * factor
        )
        for index in range(OUT_PARTS):
            block = pl.ds(index * out_rows, out_rows)
            copy = pltpu.make_async_copy(
                out_data.at[block, part], out_ref.at[block, part], out_sem.at[len(out_copies)]
            )
            copy.start()
            out_copies.append(copy)
    for copy in out_copies:
        copy.wait()


def exchange_block(at, row_parts, pieces):
    offsets, turns, rows, width = row_parts[0].shape
    col_count = pieces[0].shape[1]
    groups = 2 * len(pieces)
    depth = groups * width
    return pl.pallas_call(
        lambda *refs: exchange_kernel(*refs, factor=1.0 / depth),
        in_specs=[pl.BlockSpec(memory_space=pltpu.SMEM)]
        + [pl.BlockSpec(memory_space=pl.ANY)] * (len(row_parts) + len(pieces)),
        out_specs=pl.BlockSpec(memory_space=pl.ANY),
        out_shape=jax.ShapeDtypeStruct((rows, col_count), jnp.float32),
        scratch_shapes=[
            pltpu.VMEM((rows, depth), jnp.bfloat16),
            pltpu.VMEM((groups, col_count, width), jnp.bfloat16),
            pltpu.VMEM((rows, col_count), jnp.float32),
            pltpu.SemaphoreType.DMA((groups,)),
            pltpu.SemaphoreType.DMA((col_count // COL_LOAD, len(pieces))),
            pltpu.SemaphoreType.DMA((col_count // COL_STEP * OUT_PARTS,)),
        ],
        compiler_params=pltpu.CompilerParams(vmem_limit_bytes=EXCHANGE_LIMIT),
        name="exchange",
    )(at, *row_parts, *pieces)


def shards(tiles, tile_owner, pair_rows, pair_cols, orbitals, support):
    tiles_here, _, tile_rows, _ = tiles.shape
    aux_count = lax.axis_size(AUX_AXES)
    bas_count = lax.axis_size(BAS_AXES)
    x_count = lax.axis_size("x")
    block = lax.axis_index(AUX_AXES)
    at = [lax.axis_index(axis) for axis in ALL_AXES]
    x_place, core = at[2:]
    myself = block * bas_count + lax.axis_index(BAS_AXES)
    slots_per_source = 2 * bas_count
    rows_per_part = NBAS // tile_rows // bas_count

    owner_flat = tile_owner[:, 0]
    by_device = (aux_count * bas_count, tiles_here)
    outgoing = half_slots(
        myself[None].astype(jnp.int32),
        tiles,
        owner_flat.reshape(by_device),
        pair_cols.reshape(by_device),
        orbitals,
        support,
        aux_count,
        slots_per_source,
    )
    own = lax.all_to_all(outgoing, AUX_AXES, split_axis=0, concat_axis=0, tiled=True)

    def sources(flat):
        near = lax.dynamic_index_in_dim(flat.reshape(aux_count, x_count, 2, tiles_here), x_place, 1, keepdims=False)
        return jnp.where(core == 0, near, near[:, ::-1]).transpose(1, 0, 2)

    counts, entries = slot_entries(
        sources(owner_flat), sources(pair_rows), block, x_place, core, slots_per_source, rows_per_part
    )
    other = lax.ppermute(own, "core", SWAP)
    local = reduce_over_x(*sum_slots(counts, entries, own, other, rows_per_part))
    pieces, row_parts = gather_both(local)
    return exchange_block(jnp.stack(at).astype(jnp.int32), row_parts, pieces)


def solution(mesh):
    fine = Mesh(mesh.devices.reshape(4, 4, 4, 2), ALL_AXES)
    in_specs = (P(ALL_AXES, None, None, None), P(), P(), P(), P(), P())
    out_specs = P(AUX_AXES, BAS_AXES)
    return jax.shard_map(shards, mesh=fine, in_specs=in_specs, out_specs=out_specs, check_vma=False)
```

```python
import jax
import jax.numpy as jnp
from jax import lax
from jax.experimental import pallas as pl
from jax.experimental.pallas import tpu as pltpu
from jax.sharding import Mesh, PartitionSpec as P

NBAS = 20480
AUX_AXES = ("z", "y")
BAS_AXES = ("x", "core")
ALL_AXES = AUX_AXES + BAS_AXES
TILE_STEP = 32
COL_STEP = 256
COL_LOAD = 512
OUT_PARTS = 4
SWAP = [(0, 1), (1, 0)]
VMEM_LIMIT = 56 * 1024 * 1024
SUM_LIMIT = 24 * 1024 * 1024
EXCHANGE_LIMIT = 36 * 1024 * 1024


def half_kernel(self_ref, owner_ref, col_ref, tiles_ref, orbital_ref, support_ref, out_ref, count_ref, kept_ref):
    step = pl.program_id(0)
    aux_here, tile_rows, tile_cols = tiles_ref.shape[1:]
    orbital_count = orbital_ref.shape[0]
    width = aux_here * orbital_count
    block_count = count_ref.shape[0]
    per_block = out_ref.shape[0] // block_count

    @pl.when(step == 0)
    def _():
        for block in range(block_count):
            count_ref[block] = 0
        orbital = lax.broadcasted_iota(jnp.int32, (orbital_count, width), 0)
        column = lax.broadcasted_iota(jnp.int32, (orbital_count, width), 1)
        spread = (lax.rem(column, orbital_count) == orbital).astype(jnp.float32)
        kept_ref[...] = lax.dot_general(
            (support_ref[...] == 1).astype(jnp.float32),
            spread,
            (((0,), (0,)), ((), ())),
            preferred_element_type=jnp.float32,
        )

    row = lax.bitwise_and(self_ref[0], 7)
    lane = lax.broadcasted_iota(jnp.int32, (tile_rows, width), 1)
    height = aux_here * tile_rows
    for first in range(0, tiles_ref.shape[0], 2):
        cols = [col_ref[row, step * tiles_ref.shape[0] + first + turn] for turn in range(2)]
        chosen = [orbital_ref[:, pl.ds(pl.multiple_of(col * tile_cols, tile_cols), tile_cols)] for col in cols]
        products = lax.dot_general(
            tiles_ref[pl.ds(first, 2)].reshape(2 * height, tile_cols),
            jnp.concatenate([chosen[0]] * aux_here + [chosen[1]] * aux_here, axis=0),
            (((1,), (1,)), ((), ())),
            preferred_element_type=jnp.float32,
        )
        for turn in range(2):
            product = products[turn * height : (turn + 1) * height, turn * width : (turn + 1) * width]
            block = lax.shift_right_logical(owner_ref[row, step * tiles_ref.shape[0] + first + turn], 3)
            rank = count_ref[block]
            count_ref[block] = rank + 1
            half = product[:tile_rows]
            for aux in range(1, aux_here):
                part = product[aux * tile_rows : (aux + 1) * tile_rows]
                half = jnp.where(lane >= aux * orbital_count, part, half)
            kept = kept_ref[pl.ds(cols[turn], 1), :] > 0.5
            out_ref[block * per_block + rank] = jnp.where(kept, half, 0.0).astype(out_ref.dtype)


def half_slots(myself, tiles, owners, cols, orbitals, support, block_count, per_block):
    count, aux_here, tile_rows, tile_cols = tiles.shape
    width = aux_here * orbitals.shape[0]
    index_spec = pl.BlockSpec((8, count), lambda i, self_ref: (self_ref[0] // 8, 0), memory_space=pltpu.SMEM)
    return pl.pallas_call(
        half_kernel,
        grid_spec=pltpu.PrefetchScalarGridSpec(
            num_scalar_prefetch=1,
            grid=(count // TILE_STEP,),
            in_specs=[
                index_spec,
                index_spec,
                pl.BlockSpec((TILE_STEP, aux_here, tile_rows, tile_cols), lambda i, _: (i, 0, 0, 0)),
                pl.BlockSpec(orbitals.shape, lambda i, _: (0, 0)),
                pl.BlockSpec(support.shape, lambda i, _: (0, 0)),
            ],
            out_specs=pl.BlockSpec((block_count * per_block, tile_rows, width), lambda i, _: (0, 0, 0)),
            scratch_shapes=[
                pltpu.SMEM((block_count,), jnp.int32),
                pltpu.VMEM((support.shape[1], width), jnp.float32),
            ],
        ),
        out_shape=jax.ShapeDtypeStruct((block_count * per_block, tile_rows, width), jnp.bfloat16),
        compiler_params=pltpu.CompilerParams(vmem_limit_bytes=VMEM_LIMIT),
        name="half_transform",
    )(myself, owners, cols, tiles, orbitals, support)


def sum_kernel(count_ref, list_ref, own_ref, other_ref, *refs):
    out_refs, (total_ref, slots, sem) = refs[:-3], refs[-3:]
    copies = [
        pltpu.make_async_copy(slots_ref, slots.at[side], sem.at[side])
        for side, slots_ref in enumerate((own_ref, other_ref))
    ]
    for copy in copies:
        copy.start()
    total_ref[...] = jnp.zeros_like(total_ref)
    for side, copy in enumerate(copies):
        copy.wait()

        def add(index, carry, side=side):
            entry = list_ref[side, index]
            slot = lax.shift_right_logical(entry, 9)
            place = lax.bitwise_and(entry, 511)
            total_ref[place] += slots[side, slot].astype(jnp.float32)
            return carry

        lax.fori_loop(0, count_ref[side], add, 0)
    first = 0
    for out_ref in out_refs:
        blocks = out_ref.shape[0]
        out_ref[...] = total_ref[pl.ds(first, blocks)].astype(out_ref.dtype)
        first += blocks


def sum_slots(counts, entries, own, other, part):
    tile_shape = own.shape[1:]
    sizes = [part] + [part // 2] * 6
    places = 4 * part
    outs = pl.pallas_call(
        sum_kernel,
        in_specs=[
            pl.BlockSpec(memory_space=pltpu.SMEM),
            pl.BlockSpec(memory_space=pltpu.SMEM),
            pl.BlockSpec(memory_space=pl.ANY),
            pl.BlockSpec(memory_space=pl.ANY),
        ],
        out_specs=[pl.BlockSpec(memory_space=pltpu.VMEM)] * len(sizes),
        out_shape=[jax.ShapeDtypeStruct((size,) + tile_shape, jnp.bfloat16) for size in sizes],
        scratch_shapes=[
            pltpu.VMEM((places,) + tile_shape, jnp.float32),
            pltpu.VMEM((2,) + own.shape, jnp.bfloat16),
            pltpu.SemaphoreType.DMA((2,)),
        ],
        compiler_params=pltpu.CompilerParams(vmem_limit_bytes=SUM_LIMIT),
        name="sum_slots",
    )(counts, entries, own, other)
    return outs


def slot_entries(owners, rows, block, x_place, core, slots_per_source, rows_per_part):
    sides, sources, tiles_here = owners.shape
    hit = lax.shift_right_logical(owners, 3) == block
    mine = jnp.logical_and(hit, (rows // rows_per_part) % 2 == core)
    before = jnp.triu(jnp.ones((tiles_here, tiles_here), jnp.bfloat16), 1)
    flags = jnp.stack([hit, mine]).astype(jnp.bfloat16)
    ahead = jnp.einsum("fkst,tu->fksu", flags, before, preferred_element_type=jnp.float32).astype(jnp.int32)
    slot = jnp.arange(sources, dtype=jnp.int32)[None, :, None] * slots_per_source + ahead[0]
    part = (rows // (2 * rows_per_part) - x_place) & 3
    place = part * rows_per_part + rows % rows_per_part
    mine_counts = jnp.sum(mine.astype(jnp.int32), axis=2)
    earlier = jnp.cumsum(mine_counts, axis=1) - mine_counts
    position = jnp.where(mine, ahead[1] + earlier[:, :, None], -1).reshape(sides, 1, sources * tiles_here)
    packed = (slot * 512 + place).reshape(sides, 1, sources * tiles_here)
    wanted = jnp.arange(sources * slots_per_source, dtype=jnp.int32)[None, :, None]
    entries = jnp.sum(jnp.where(position == wanted, packed, 0), axis=2)
    return jnp.sum(mine_counts, axis=1), entries


def shift(value, axis, by):
    return lax.ppermute(value, axis, [(i, (i + by) % 4) for i in range(4)])


def reduce_over_x(own, p1a, p1b, p2a, p2b, p3a, p3b):
    def add(*values):
        total = sum(value.astype(jnp.float32) for value in values).astype(jnp.bfloat16)
        return total.reshape(-1, total.shape[-1])

    far_a, far_b = shift(p2a, "x", 1), shift(p2b, "x", -1)
    low_b, high_a = shift(p1b, "x", 1), shift(p3a, "x", -1)
    low_a = shift(add(p1a, far_a).reshape(p1a.shape), "x", 1)
    high_b = shift(add(p3b, far_b).reshape(p3b.shape), "x", -1)
    low, high = jnp.concatenate([low_a, low_b]), jnp.concatenate([high_a, high_b])
    return add(own, low, high)


def device(z, y, x, core):
    return ((z * 4 + y) * 4 + x) * 2 + core


def shift_turned(value, second, by):
    pairs = []
    for z in range(4):
        for y in range(4):
            for x in range(4):
                for core in range(2):
                    along_z = (core == 0) != second
                    to_z, to_y = ((z + by) % 4, y) if along_z else (z, (y + by) % 4)
                    pairs.append((device(z, y, x, core), device(to_z, to_y, x, core)))
    return lax.ppermute(value, ALL_AXES, pairs)


def spread_pairs(turn):
    along_x, along_zy = [], []
    for zg in range(4):
        for yg in range(4):
            for z in range(4):
                for high in range(2):
                    y = 2 * high + (yg // 2 ^ turn)
                    x = (zg + y + z) % 4
                    along_x.append((device(zg, yg, z, high), device(zg, yg, x, high)))
                    along_zy.append((device(zg, yg, x, high), device(z, y, x, yg % 2)))
    return along_x, along_zy


def gather_both(local):
    stage = lax.optimization_barrier
    middle = local.shape[0] // 2
    turned = lax.axis_index("y") // 2 == 1
    halves = local[:middle], local[middle:]
    pairs = [spread_pairs(turn) for turn in range(2)]

    low, high = shift_turned(local, False, 1), shift_turned(local, False, -1)
    rows = [lax.ppermute(jnp.where(turned, halves[1 - t], halves[t]), ALL_AXES, pairs[t][0]) for t in range(2)]
    low, high, rows = stage((low, high, rows))

    far_a, far_b = shift_turned(high[:middle], False, -1), shift_turned(low[middle:], False, 1)
    near = jnp.stack([local, low])
    near_low, near_high = shift_turned(near, True, 1), shift_turned(near, True, -1)
    rows = jnp.stack([lax.ppermute(rows[t], ALL_AXES, pairs[t][1]) for t in range(2)])
    far = jnp.stack([high, jnp.concatenate([far_a, far_b])])
    near_low, near_high, far, rows = stage((near_low, near_high, far, rows))

    rows_low, rows_high = shift(rows, "x", 1), shift(rows, "x", -1)
    far_low, far_high = shift_turned(far, True, 1), shift_turned(far, True, -1)
    far_low, far_high, rows_low, rows_high = stage((far_low, far_high, rows_low, rows_high))

    near_far, far_far = shift_turned(near_high, True, -1), shift_turned(far_low, True, 1)
    rows_far = jnp.stack([shift(rows_high[0], "x", -1), shift(rows_low[1], "x", 1)])
    rows_near, rows_far = jnp.stack([rows, rows_low]), jnp.stack([rows_high, rows_far])
    rows = [rows_near, rows_far, lax.ppermute(rows_near, "core", SWAP), lax.ppermute(rows_far, "core", SWAP)]
    return [near, far, near_low, far_low, near_high, far_high, near_far, far_far], rows


def exchange_kernel(at_ref, *refs, factor):
    row_refs, col_refs = refs[:4], refs[4:12]
    out_ref, row_data, col_data, out_data, row_sem, col_sem, out_sem = refs[12:]
    width = col_data.shape[-1]
    rows, col_count = out_data.shape
    z_place, y_place, x_place, core = (at_ref[i] for i in range(4))

    def order(offset):
        odd = lax.bitwise_and(offset, 1)
        half = lax.shift_right_logical(offset, 1)
        return jnp.where(odd == 1, 2 - half, offset + half)

    row_copies = []
    for core_from, pair in ((core, row_refs[:2]), (1 - core, row_refs[2:])):
        for index, offset in enumerate((0, -1, 1, 2)):
            for turn in range(2):
                zg = lax.bitwise_and(x_place + offset - y_place - z_place, 3)
                yg = 2 * lax.bitwise_xor(lax.bitwise_and(y_place, 1), turn) + core_from
                z_at = order(lax.bitwise_and(zg - z_place, 3))
                y_at = order(lax.bitwise_and(yg - y_place, 3))
                place = jnp.where(core == 0, 4 * y_at + z_at, 4 * z_at + y_at)
                row_copies.append(
                    pltpu.make_async_copy(
                        pair[index // 2].at[index % 2, turn],
                        row_data.at[:, pl.ds(pl.multiple_of(place * width, width), width)],
                        row_sem.at[len(row_copies)],
                    )
                )
    col_copies = []
    for first in range(0, col_count, COL_LOAD):
        part = pl.ds(first, COL_LOAD)
        col_copies.append(
            [
                pltpu.make_async_copy(
                    col_ref.at[:, part],
                    col_data.at[pl.ds(2 * index, 2), part],
                    col_sem.at[len(col_copies), index],
                )
                for index, col_ref in enumerate(col_refs)
            ]
        )
    for copy in row_copies + sum(col_copies, []):
        copy.start()
    for copy in row_copies:
        copy.wait()

    out_copies = []
    out_rows = rows // OUT_PARTS
    for first in range(0, col_count, COL_STEP):
        if first % COL_LOAD == 0:
            for copy in col_copies[first // COL_LOAD]:
                copy.wait()
        part = pl.ds(first, COL_STEP)
        columns = jnp.concatenate([col_data[group, part] for group in range(col_data.shape[0])], axis=1)
        out_data[:, part] = (
            lax.dot_general(
                row_data[...], columns, (((1,), (1,)), ((), ())), preferred_element_type=jnp.float32
            )
            * factor
        )
        for index in range(OUT_PARTS):
            block = pl.ds(index * out_rows, out_rows)
            copy = pltpu.make_async_copy(
                out_data.at[block, part], out_ref.at[block, part], out_sem.at[len(out_copies)]
            )
            copy.start()
            out_copies.append(copy)
    for copy in out_copies:
        copy.wait()


def exchange_block(at, row_parts, pieces):
    offsets, turns, rows, width = row_parts[0].shape
    col_count = pieces[0].shape[1]
    groups = 2 * len(pieces)
    depth = groups * width
    return pl.pallas_call(
        lambda *refs: exchange_kernel(*refs, factor=1.0 / depth),
        in_specs=[pl.BlockSpec(memory_space=pltpu.SMEM)]
        + [pl.BlockSpec(memory_space=pl.ANY)] * (len(row_parts) + len(pieces)),
        out_specs=pl.BlockSpec(memory_space=pl.ANY),
        out_shape=jax.ShapeDtypeStruct((rows, col_count), jnp.float32),
        scratch_shapes=[
            pltpu.VMEM((rows, depth), jnp.bfloat16),
            pltpu.VMEM((groups, col_count, width), jnp.bfloat16),
            pltpu.VMEM((rows, col_count), jnp.float32),
            pltpu.SemaphoreType.DMA((groups,)),
            pltpu.SemaphoreType.DMA((col_count // COL_LOAD, len(pieces))),
            pltpu.SemaphoreType.DMA((col_count // COL_STEP * OUT_PARTS,)),
        ],
        compiler_params=pltpu.CompilerParams(vmem_limit_bytes=EXCHANGE_LIMIT),
        name="exchange",
    )(at, *row_parts, *pieces)


def shards(tiles, tile_owner, pair_rows, pair_cols, orbitals, support):
    tiles_here, _, tile_rows, _ = tiles.shape
    aux_count = lax.axis_size(AUX_AXES)
    bas_count = lax.axis_size(BAS_AXES)
    x_count = lax.axis_size("x")
    block = lax.axis_index(AUX_AXES)
    at = [lax.axis_index(axis) for axis in ALL_AXES]
    x_place, core = at[2:]
    myself = block * bas_count + lax.axis_index(BAS_AXES)
    slots_per_source = 2 * bas_count
    rows_per_part = NBAS // tile_rows // bas_count

    owner_flat = tile_owner[:, 0]
    by_device = (aux_count * bas_count, tiles_here)
    outgoing = half_slots(
        myself[None].astype(jnp.int32),
        tiles,
        owner_flat.reshape(by_device),
        pair_cols.reshape(by_device),
        orbitals,
        support,
        aux_count,
        slots_per_source,
    )
    own = lax.all_to_all(outgoing, AUX_AXES, split_axis=0, concat_axis=0, tiled=True)

    def sources(flat):
        near = lax.dynamic_index_in_dim(flat.reshape(aux_count, x_count, 2, tiles_here), x_place, 1, keepdims=False)
        return jnp.where(core == 0, near, near[:, ::-1]).transpose(1, 0, 2)

    counts, entries = slot_entries(
        sources(owner_flat), sources(pair_rows), block, x_place, core, slots_per_source, rows_per_part
    )
    other = lax.ppermute(own, "core", SWAP)
    local = reduce_over_x(*sum_slots(counts, entries, own, other, rows_per_part))
    pieces, row_parts = gather_both(local)
    return exchange_block(jnp.stack(at).astype(jnp.int32), row_parts, pieces)


def solution(mesh):
    fine = Mesh(mesh.devices.reshape(4, 4, 4, 2), ALL_AXES)
    in_specs = (P(ALL_AXES, None, None, None), P(), P(), P(), P(), P())
    out_specs = P(AUX_AXES, BAS_AXES)
    return jax.shard_map(shards, mesh=fine, in_specs=in_specs, out_specs=out_specs, check_vma=False)
```

```python
import jax
import jax.numpy as jnp
from jax import lax
from jax.experimental import pallas as pl
from jax.experimental.pallas import tpu as pltpu
from jax.sharding import Mesh, PartitionSpec as P

NBAS = 20480
AUX_AXES = ("z", "y")
BAS_AXES = ("x", "core")
ALL_AXES = AUX_AXES + BAS_AXES
TILE_STEP = 32
COL_STEP = 256
COL_LOAD = 512
OUT_PARTS = 4
SWAP = [(0, 1), (1, 0)]
VMEM_LIMIT = 56 * 1024 * 1024
SUM_LIMIT = 24 * 1024 * 1024
EXCHANGE_LIMIT = 36 * 1024 * 1024


def half_kernel(self_ref, owner_ref, col_ref, tiles_ref, orbital_ref, support_ref, out_ref, count_ref, kept_ref):
    step = pl.program_id(0)
    aux_here, tile_rows, tile_cols = tiles_ref.shape[1:]
    orbital_count = orbital_ref.shape[0]
    width = aux_here * orbital_count
    block_count = count_ref.shape[0]
    per_block = out_ref.shape[0] // block_count

    @pl.when(step == 0)
    def _():
        for block in range(block_count):
            count_ref[block] = 0
        orbital = lax.broadcasted_iota(jnp.int32, (orbital_count, width), 0)
        column = lax.broadcasted_iota(jnp.int32, (orbital_count, width), 1)
        spread = (lax.rem(column, orbital_count) == orbital).astype(jnp.float32)
        kept_ref[...] = lax.dot_general(
            (support_ref[...] == 1).astype(jnp.float32),
            spread,
            (((0,), (0,)), ((), ())),
            preferred_element_type=jnp.float32,
        )

    row = lax.bitwise_and(self_ref[0], 7)
    lane = lax.broadcasted_iota(jnp.int32, (tile_rows, width), 1)
    height = aux_here * tile_rows
    for first in range(0, tiles_ref.shape[0], 2):
        cols = [col_ref[row, step * tiles_ref.shape[0] + first + turn] for turn in range(2)]
        chosen = [orbital_ref[:, pl.ds(pl.multiple_of(col * tile_cols, tile_cols), tile_cols)] for col in cols]
        products = lax.dot_general(
            tiles_ref[pl.ds(first, 2)].reshape(2 * height, tile_cols),
            jnp.concatenate([chosen[0]] * aux_here + [chosen[1]] * aux_here, axis=0),
            (((1,), (1,)), ((), ())),
            preferred_element_type=jnp.float32,
        )
        for turn in range(2):
            product = products[turn * height : (turn + 1) * height, turn * width : (turn + 1) * width]
            block = lax.shift_right_logical(owner_ref[row, step * tiles_ref.shape[0] + first + turn], 3)
            rank = count_ref[block]
            count_ref[block] = rank + 1
            half = product[:tile_rows]
            for aux in range(1, aux_here):
                part = product[aux * tile_rows : (aux + 1) * tile_rows]
                half = jnp.where(lane >= aux * orbital_count, part, half)
            kept = kept_ref[pl.ds(cols[turn], 1), :] > 0.5
            out_ref[block * per_block + rank] = jnp.where(kept, half, 0.0).astype(out_ref.dtype)


def half_slots(myself, tiles, owners, cols, orbitals, support, block_count, per_block):
    count, aux_here, tile_rows, tile_cols = tiles.shape
    width = aux_here * orbitals.shape[0]
    index_spec = pl.BlockSpec((8, count), lambda i, self_ref: (self_ref[0] // 8, 0), memory_space=pltpu.SMEM)
    return pl.pallas_call(
        half_kernel,
        grid_spec=pltpu.PrefetchScalarGridSpec(
            num_scalar_prefetch=1,
            grid=(count // TILE_STEP,),
            in_specs=[
                index_spec,
                index_spec,
                pl.BlockSpec((TILE_STEP, aux_here, tile_rows, tile_cols), lambda i, _: (i, 0, 0, 0)),
                pl.BlockSpec(orbitals.shape, lambda i, _: (0, 0)),
                pl.BlockSpec(support.shape, lambda i, _: (0, 0)),
            ],
            out_specs=pl.BlockSpec((block_count * per_block, tile_rows, width), lambda i, _: (0, 0, 0)),
            scratch_shapes=[
                pltpu.SMEM((block_count,), jnp.int32),
                pltpu.VMEM((support.shape[1], width), jnp.float32),
            ],
        ),
        out_shape=jax.ShapeDtypeStruct((block_count * per_block, tile_rows, width), jnp.bfloat16),
        compiler_params=pltpu.CompilerParams(vmem_limit_bytes=VMEM_LIMIT),
        name="half_transform",
    )(myself, owners, cols, tiles, orbitals, support)


def sum_kernel(count_ref, list_ref, own_ref, other_ref, *refs):
    out_refs, (total_ref, slots, sem) = refs[:-3], refs[-3:]
    copies = [
        pltpu.make_async_copy(slots_ref, slots.at[side], sem.at[side])
        for side, slots_ref in enumerate((own_ref, other_ref))
    ]
    for copy in copies:
        copy.start()
    total_ref[...] = jnp.zeros_like(total_ref)
    for side, copy in enumerate(copies):
        copy.wait()

        def add(index, carry, side=side):
            entry = list_ref[side, index]
            slot = lax.shift_right_logical(entry, 9)
            place = lax.bitwise_and(entry, 511)
            total_ref[place] += slots[side, slot].astype(jnp.float32)
            return carry

        lax.fori_loop(0, count_ref[side], add, 0)
    first = 0
    for out_ref in out_refs:
        blocks = out_ref.shape[0]
        out_ref[...] = total_ref[pl.ds(first, blocks)].astype(out_ref.dtype)
        first += blocks


def sum_slots(counts, entries, own, other, part):
    tile_shape = own.shape[1:]
    sizes = [part] + [part // 2] * 6
    places = 4 * part
    outs = pl.pallas_call(
        sum_kernel,
        in_specs=[
            pl.BlockSpec(memory_space=pltpu.SMEM),
            pl.BlockSpec(memory_space=pltpu.SMEM),
            pl.BlockSpec(memory_space=pl.ANY),
            pl.BlockSpec(memory_space=pl.ANY),
        ],
        out_specs=[pl.BlockSpec(memory_space=pltpu.VMEM)] * len(sizes),
        out_shape=[jax.ShapeDtypeStruct((size,) + tile_shape, jnp.bfloat16) for size in sizes],
        scratch_shapes=[
            pltpu.VMEM((places,) + tile_shape, jnp.float32),
            pltpu.VMEM((2,) + own.shape, jnp.bfloat16),
            pltpu.SemaphoreType.DMA((2,)),
        ],
        compiler_params=pltpu.CompilerParams(vmem_limit_bytes=SUM_LIMIT),
        name="sum_slots",
    )(counts, entries, own, other)
    return outs


def slot_entries(owners, rows, block, x_place, core, slots_per_source, rows_per_part):
    sides, sources, tiles_here = owners.shape
    hit = lax.shift_right_logical(owners, 3) == block
    mine = jnp.logical_and(hit, (rows // rows_per_part) % 2 == core)
    before = jnp.triu(jnp.ones((tiles_here, tiles_here), jnp.bfloat16), 1)
    flags = jnp.stack([hit, mine]).astype(jnp.bfloat16)
    ahead = jnp.einsum("fkst,tu->fksu", flags, before, preferred_element_type=jnp.float32).astype(jnp.int32)
    slot = jnp.arange(sources, dtype=jnp.int32)[None, :, None] * slots_per_source + ahead[0]
    part = (rows // (2 * rows_per_part) - x_place) & 3
    place = part * rows_per_part + rows % rows_per_part
    mine_counts = jnp.sum(mine.astype(jnp.int32), axis=2)
    earlier = jnp.cumsum(mine_counts, axis=1) - mine_counts
    position = jnp.where(mine, ahead[1] + earlier[:, :, None], -1).reshape(sides, 1, sources * tiles_here)
    packed = (slot * 512 + place).reshape(sides, 1, sources * tiles_here)
    wanted = jnp.arange(sources * slots_per_source, dtype=jnp.int32)[None, :, None]
    entries = jnp.sum(jnp.where(position == wanted, packed, 0), axis=2)
    return jnp.sum(mine_counts, axis=1), entries


def shift(value, axis, by):
    return lax.ppermute(value, axis, [(i, (i + by) % 4) for i in range(4)])


def reduce_over_x(own, p1a, p1b, p2a, p2b, p3a, p3b):
    def add(*values):
        total = sum(value.astype(jnp.float32) for value in values).astype(jnp.bfloat16)
        return total.reshape(-1, total.shape[-1])

    far_a, far_b = shift(p2a, "x", 1), shift(p2b, "x", -1)
    low_b, high_a = shift(p1b, "x", 1), shift(p3a, "x", -1)
    low_a = shift(add(p1a, far_a).reshape(p1a.shape), "x", 1)
    high_b = shift(add(p3b, far_b).reshape(p3b.shape), "x", -1)
    low, high = jnp.concatenate([low_a, low_b]), jnp.concatenate([high_a, high_b])
    return add(own, low, high)


def device(z, y, x, core):
    return ((z * 4 + y) * 4 + x) * 2 + core


def shift_turned(value, second, by):
    pairs = []
    for z in range(4):
        for y in range(4):
            for x in range(4):
                for core in range(2):
                    along_z = (core == 0) != second
                    to_z, to_y = ((z + by) % 4, y) if along_z else (z, (y + by) % 4)
                    pairs.append((device(z, y, x, core), device(to_z, to_y, x, core)))
    return lax.ppermute(value, ALL_AXES, pairs)


def spread_pairs(turn):
    along_x, along_zy = [], []
    for zg in range(4):
        for yg in range(4):
            for z in range(4):
                for high in range(2):
                    y = 2 * high + (yg // 2 ^ turn)
                    x = (zg + y + z) % 4
                    along_x.append((device(zg, yg, z, high), device(zg, yg, x, high)))
                    along_zy.append((device(zg, yg, x, high), device(z, y, x, yg % 2)))
    return along_x, along_zy


def gather_both(local):
    stage = lax.optimization_barrier
    middle = local.shape[0] // 2
    turned = lax.axis_index("y") // 2 == 1
    halves = local[:middle], local[middle:]
    pairs = [spread_pairs(turn) for turn in range(2)]

    low, high = shift_turned(local, False, 1), shift_turned(local, False, -1)
    rows = [lax.ppermute(jnp.where(turned, halves[1 - t], halves[t]), ALL_AXES, pairs[t][0]) for t in range(2)]
    low, high, rows = stage((low, high, rows))

    far_a, far_b = shift_turned(high[:middle], False, -1), shift_turned(low[middle:], False, 1)
    near = jnp.stack([local, low])
    near_low, near_high = shift_turned(near, True, 1), shift_turned(near, True, -1)
    rows = jnp.stack([lax.ppermute(rows[t], ALL_AXES, pairs[t][1]) for t in range(2)])
    far = jnp.stack([high, jnp.concatenate([far_a, far_b])])
    near_low, near_high, far, rows = stage((near_low, near_high, far, rows))

    rows_low, rows_high = shift(rows, "x", 1), shift(rows, "x", -1)
    far_low, far_high = shift_turned(far, True, 1), shift_turned(far, True, -1)
    far_low, far_high, rows_low, rows_high = stage((far_low, far_high, rows_low, rows_high))

    near_far, far_far = shift_turned(near_high, True, -1), shift_turned(far_low, True, 1)
    rows_far = jnp.stack([shift(rows_high[0], "x", -1), shift(rows_low[1], "x", 1)])
    rows_near, rows_far = jnp.stack([rows, rows_low]), jnp.stack([rows_high, rows_far])
    rows = [rows_near, rows_far, lax.ppermute(rows_near, "core", SWAP), lax.ppermute(rows_far, "core", SWAP)]
    return [near, far, near_low, far_low, near_high, far_high, near_far, far_far], rows


def exchange_kernel(at_ref, *refs, factor):
    row_refs, col_refs = refs[:4], refs[4:12]
    out_ref, row_data, col_data, out_data, row_sem, col_sem, out_sem = refs[12:]
    width = col_data.shape[-1]
    rows, col_count = out_data.shape
    z_place, y_place, x_place, core = (at_ref[i] for i in range(4))

    def order(offset):
        odd = lax.bitwise_and(offset, 1)
        half = lax.shift_right_logical(offset, 1)
        return jnp.where(odd == 1, 2 - half, offset + half)

    row_copies = []
    for core_from, pair in ((core, row_refs[:2]), (1 - core, row_refs[2:])):
        for index, offset in enumerate((0, -1, 1, 2)):
            for turn in range(2):
                zg = lax.bitwise_and(x_place + offset - y_place - z_place, 3)
                yg = 2 * lax.bitwise_xor(lax.bitwise_and(y_place, 1), turn) + core_from
                z_at = order(lax.bitwise_and(zg - z_place, 3))
                y_at = order(lax.bitwise_and(yg - y_place, 3))
                place = jnp.where(core == 0, 4 * y_at + z_at, 4 * z_at + y_at)
                row_copies.append(
                    pltpu.make_async_copy(
                        pair[index // 2].at[index % 2, turn],
                        row_data.at[:, pl.ds(pl.multiple_of(place * width, width), width)],
                        row_sem.at[len(row_copies)],
                    )
                )
    col_copies = []
    for first in range(0, col_count, COL_LOAD):
        part = pl.ds(first, COL_LOAD)
        col_copies.append(
            [
                pltpu.make_async_copy(
                    col_ref.at[:, part],
                    col_data.at[pl.ds(2 * index, 2), part],
                    col_sem.at[len(col_copies), index],
                )
                for index, col_ref in enumerate(col_refs)
            ]
        )
    for copy in row_copies + col_copies[0]:
        copy.start()
    for copy in row_copies:
        copy.wait()
    for copy in sum(col_copies[1:], []):
        copy.start()

    out_copies = []
    out_rows = rows // OUT_PARTS
    for first in range(0, col_count, COL_STEP):
        if first % COL_LOAD == 0:
            for copy in col_copies[first // COL_LOAD]:
                copy.wait()
        part = pl.ds(first, COL_STEP)
        columns = jnp.concatenate([col_data[group, part] for group in range(col_data.shape[0])], axis=1)
        out_data[:, part] = (
            lax.dot_general(
                row_data[...], columns, (((1,), (1,)), ((), ())), preferred_element_type=jnp.float32
            )
            * factor
        )
        for index in range(OUT_PARTS):
            block = pl.ds(index * out_rows, out_rows)
            copy = pltpu.make_async_copy(
                out_data.at[block, part], out_ref.at[block, part], out_sem.at[len(out_copies)]
            )
            copy.start()
            out_copies.append(copy)
    for copy in out_copies:
        copy.wait()


def exchange_block(at, row_parts, pieces):
    offsets, turns, rows, width = row_parts[0].shape
    col_count = pieces[0].shape[1]
    groups = 2 * len(pieces)
    depth = groups * width
    return pl.pallas_call(
        lambda *refs: exchange_kernel(*refs, factor=1.0 / depth),
        in_specs=[pl.BlockSpec(memory_space=pltpu.SMEM)]
        + [pl.BlockSpec(memory_space=pl.ANY)] * (len(row_parts) + len(pieces)),
        out_specs=pl.BlockSpec(memory_space=pl.ANY),
        out_shape=jax.ShapeDtypeStruct((rows, col_count), jnp.float32),
        scratch_shapes=[
            pltpu.VMEM((rows, depth), jnp.bfloat16),
            pltpu.VMEM((groups, col_count, width), jnp.bfloat16),
            pltpu.VMEM((rows, col_count), jnp.float32),
            pltpu.SemaphoreType.DMA((groups,)),
            pltpu.SemaphoreType.DMA((col_count // COL_LOAD, len(pieces))),
            pltpu.SemaphoreType.DMA((col_count // COL_STEP * OUT_PARTS,)),
        ],
        compiler_params=pltpu.CompilerParams(vmem_limit_bytes=EXCHANGE_LIMIT),
        name="exchange",
    )(at, *row_parts, *pieces)


def shards(tiles, tile_owner, pair_rows, pair_cols, orbitals, support):
    tiles_here, _, tile_rows, _ = tiles.shape
    aux_count = lax.axis_size(AUX_AXES)
    bas_count = lax.axis_size(BAS_AXES)
    x_count = lax.axis_size("x")
    block = lax.axis_index(AUX_AXES)
    at = [lax.axis_index(axis) for axis in ALL_AXES]
    x_place, core = at[2:]
    myself = block * bas_count + lax.axis_index(BAS_AXES)
    slots_per_source = 2 * bas_count
    rows_per_part = NBAS // tile_rows // bas_count

    owner_flat = tile_owner[:, 0]
    by_device = (aux_count * bas_count, tiles_here)
    outgoing = half_slots(
        myself[None].astype(jnp.int32),
        tiles,
        owner_flat.reshape(by_device),
        pair_cols.reshape(by_device),
        orbitals,
        support,
        aux_count,
        slots_per_source,
    )
    own = lax.all_to_all(outgoing, AUX_AXES, split_axis=0, concat_axis=0, tiled=True)

    def sources(flat):
        near = lax.dynamic_index_in_dim(flat.reshape(aux_count, x_count, 2, tiles_here), x_place, 1, keepdims=False)
        return jnp.where(core == 0, near, near[:, ::-1]).transpose(1, 0, 2)

    counts, entries = slot_entries(
        sources(owner_flat), sources(pair_rows), block, x_place, core, slots_per_source, rows_per_part
    )
    other = lax.ppermute(own, "core", SWAP)
    local = reduce_over_x(*sum_slots(counts, entries, own, other, rows_per_part))
    pieces, row_parts = gather_both(local)
    return exchange_block(jnp.stack(at).astype(jnp.int32), row_parts, pieces)


def solution(mesh):
    fine = Mesh(mesh.devices.reshape(4, 4, 4, 2), ALL_AXES)
    in_specs = (P(ALL_AXES, None, None, None), P(), P(), P(), P(), P())
    out_specs = P(AUX_AXES, BAS_AXES)
    return jax.shard_map(shards, mesh=fine, in_specs=in_specs, out_specs=out_specs, check_vma=False)
```
